512 devices in a mesh: users: 128 (over z, x, core), items: 4 (over y).
Axes of the slice: x: 4, y: 4, z: 16, core: 2. Of those that a mesh axis runs over, the one named last changes fastest.
Arguments:
- tile_users: int32 [128, 4, 128], P('users', 'items'), may hold values from 0 to 127
- tile_owners: int32 [128, 4, 128, 1], P('users', 'items'), may hold values from 0 to 127; in each aligned block of 128 rows (0 to 127, 128 to 255, ..., all dimensions but the last counted through in order) at most 2 rows name the same one
- tile_blocks: int32 [128, 4, 128], P('users', 'items'), may hold values from 0 to 3
- tile_contexts: int32 [128, 4, 128], P('users', 'items'), may hold values from 0 to 7
- row_users: int32 [128, 4, 128, 128], P('users', 'items'), may hold values from 0 to 15
- row_items: int32 [128, 4, 128, 128], P('users', 'items'), may hold values from 0 to 15
- row_contexts: int32 [128, 4, 128, 128], P('users', 'items'), may hold values from 0 to 127
- tile_values: bfloat16 [128, 4, 128, 128], P('users', 'items'), may hold values from -49152 to 49152
- tile_count: int32 [128, 4], P('users', 'items'), may hold values from 64 to 128, as said below
- item_factors: bfloat16 [8192, 256], P('users'), may hold values from -0.125 to 0.25
- context_factors: bfloat16 [1024, 256], replicated, may hold values from -0.125 to 0.25
- profile: bfloat16 [262144, 2048], P('users', 'items'), may hold values from -192 to 192
- feature_factors: bfloat16 [2048, 256], P('items'), may hold values from -6 to 6
Outputs:
- user_factors: bfloat16 [262144, 256], P('users')
- feature_new: bfloat16 [2048, 256], P('items')
The draws below stay inside these ranges and needn't reach their ends.
Inputs may be any that keep to these rules, and one draw needn't show every extreme that they name: On one device at most 2 tiles name one index of users in tile_owners, a bound that some block reaches. The live tiles of a device are its first tile_count tiles; some device has all 128 live.
All inputs are finite; a program needn't handle non-finite values.
Results may differ from the reference program's by a relative error of at most 0.00155.
The reference program's roundings to bfloat16 on the way count: a program that leaves them out, or rounds other values in their place, can miss the bound.
Values may be sent and summed in bfloat16 or wider, within the bound.
A program may use at most 64 MiB of HBM per device.

```python
import math
import jax
import jax.numpy as jnp
import numpy as np
from jax import lax

R = 256
FEAT = 2048
CTX = 1024
CB = 128
IB = 16
UB = 16
TR = 128
U_DEV = 2048
TILES_DEV = 128
CAP = 2
BLK_OWN = 4
USERS = 262144
NI = 8192
N_USERS = 128
N_ITEMS = 4


def draw_tile_count(key, part):
    first_key, second_key = jax.random.split(jax.random.fold_in(key, 17))
    divisor_table = jnp.array([1, 1, 1, 2], dtype=jnp.int32)
    picks = jax.random.randint(first_key, (N_USERS * N_ITEMS,), 0, 4)
    counts = TILES_DEV // divisor_table[picks]
    full_at = jax.random.randint(second_key, (), 0, N_USERS * N_ITEMS)
    counts = jnp.where(jnp.arange(N_USERS * N_ITEMS) == full_at, TILES_DEV, counts)
    return counts.reshape(N_USERS, N_ITEMS).astype(jnp.int32)


def with_ends(values, stream_key, smallest, high):
    longest = values.shape.index(max(values.shape))
    spots = []
    for shift in (0, 1):
        where = [jax.random.randint(jax.random.fold_in(stream_key, axis), (), 0, length) for axis, length in enumerate(values.shape)]
        where[longest] = (where[longest] + shift) % values.shape[longest]
        spots.append(tuple(where))
    return values.at[spots[0]].set(smallest).at[spots[1]].set(high)


def steps_of(own_key, extent, cuts, least, high):
    factor_of = 1.0
    for axis_at, shards_of in cuts:
        draws = jax.random.uniform(jax.random.fold_in(jax.random.fold_in(own_key, 6), axis_at), (shards_of,), jnp.float32, least / len(cuts), high / len(cuts))
        factor_of = factor_of * jnp.repeat(jnp.exp(draws), extent[axis_at] // shards_of).reshape((-1,) + (1,) * (len(extent) - 1 - axis_at))
    return factor_of


def shared_out(stream_key, own, number, rows, number_of, top, most, skew):
    order = jax.random.permutation(stream_key, number_of)
    crowded, ordinary = portions_of(number_of, rows * top, most, skew, True), portions_of(number_of, rows * top, most, skew, False)
    places = jnp.arange(number_of)

    def named(sizes, offset_by):
        used = int((sizes > 0).sum())
        fixed = max(1, used // 4)
        passed = fixed + (places - fixed + offset_by * (used - fixed)) % max(1, number_of - fixed)
        return jnp.zeros((number_of,), jnp.int32).at[order[jnp.where(places < fixed, places, passed)]].set(jnp.asarray(sizes, jnp.int32))

    sizes = jnp.where(number % 4 == 0, named(crowded, number // 4), named(ordinary, number - number // 4 - 1))
    mixed = jax.random.permutation(jax.random.fold_in(own, 3), number_of)
    source_of, sink = mixed[0:number_of // 2 * 2:2], mixed[1:number_of // 2 * 2:2]
    slack = jnp.minimum(sizes[source_of] - 1, most - sizes[sink]) // 2
    slack = jnp.where((source_of == order[0]) | (sink == order[0]) | (sizes[sink] == 0), 0, jnp.maximum(slack, 0))
    passed = jax.random.randint(jax.random.fold_in(own, 4), (number_of // 2,), 0, 1 << 20) % (slack + 1)
    sizes = sizes.at[source_of].add(-passed).at[sink].add(passed)
    members = jnp.searchsorted(jnp.cumsum(sizes), jnp.arange(rows * top), side="right").astype(jnp.int32)
    grid = members.reshape(top, rows).T
    grid = grid[jax.random.permutation(jax.random.fold_in(own, 1), rows)]
    offset_by = jax.random.randint(jax.random.fold_in(own, 2), (rows, 1), 0, top)
    return jnp.take_along_axis(grid, (jnp.arange(top)[None, :] + offset_by) % top, axis=1)


def portions_of(amount, total, limit, slope, full):
    weights = [(1 << 20) // math.isqrt(grade ** slope) + 1 for grade in range(1, amount + 1)]
    largest = limit if full else min(limit, max(-(-total // amount), total * weights[0] // sum(weights)))
    least = 1 if total - largest >= amount - 1 else 0
    given, spare = [largest] + [least] * (amount - 1), total - largest - least * (amount - 1)
    while spare > 0:
        movable = [i for i in range(1, amount) if given[i] < largest] or [i for i in range(1, amount) if given[i] < limit]
        whole, remaining = sum([weights[i] for i in movable]), spare
        for i in movable:
            more = min(limit - given[i], max(1, remaining * weights[i] // whole), spare)
            given[i] = given[i] + more
            spare = spare - more
    return np.array(given)


def centred(rng, shape, scale, bound, shards=(), kind=jnp.bfloat16):
    result = scale * jax.random.normal(rng, shape, jnp.float32)
    if shards:
        result = result * steps_of(rng, shape, shards, -0.22, 0.18)
    return jnp.clip(result, -bound, bound).astype(kind)


def setup_inputs(seed: int = 0) -> dict:
    key_of = jax.random.split(jax.random.key(seed), 14)
    tile_users = with_ends(jax.random.randint(key_of[0], (N_USERS, N_ITEMS, TILES_DEV), 0, U_DEV // UB), jax.random.fold_in(key_of[0], 1), 0, (U_DEV // UB) - 1).astype(jnp.int32)
    tile_owners_keys = jax.random.split(jax.random.fold_in(key_of[1], 1), N_USERS * N_ITEMS * TILES_DEV // TILES_DEV)
    tile_owners_turns = jax.random.permutation(jax.random.fold_in(key_of[1], 3), N_USERS * N_ITEMS * TILES_DEV // TILES_DEV)
    tile_owners = jax.vmap(lambda own, number: shared_out(jax.random.fold_in(key_of[1], 2), own, number, TILES_DEV, N_USERS, 1, CAP, 2))(tile_owners_keys, tile_owners_turns).reshape((N_USERS, N_ITEMS, TILES_DEV, 1))
    tile_blocks = with_ends(jax.random.randint(key_of[2], (N_USERS, N_ITEMS, TILES_DEV), 0, BLK_OWN), jax.random.fold_in(key_of[2], 1), 0, BLK_OWN - 1).astype(jnp.int32)
    tile_contexts = with_ends(jax.random.randint(key_of[3], (N_USERS, N_ITEMS, TILES_DEV), 0, CTX // CB), jax.random.fold_in(key_of[3], 1), 0, (CTX // CB) - 1).astype(jnp.int32)
    row_users = with_ends(jax.random.randint(key_of[4], (N_USERS, N_ITEMS, TILES_DEV, TR), 0, UB), jax.random.fold_in(key_of[4], 1), 0, UB - 1).astype(jnp.int32)
    row_items = with_ends(jax.random.randint(key_of[5], (N_USERS, N_ITEMS, TILES_DEV, TR), 0, IB), jax.random.fold_in(key_of[5], 1), 0, IB - 1).astype(jnp.int32)
    row_contexts = with_ends(jax.random.randint(key_of[6], (N_USERS, N_ITEMS, TILES_DEV, TR), 0, CB), jax.random.fold_in(key_of[6], 1), 0, CB - 1).astype(jnp.int32)
    tile_values = centred(key_of[7], (N_USERS, N_ITEMS, TILES_DEV, TR), 8192.0, 49152.0, ((0, 128), (1, 4)))
    tile_count = draw_tile_count(jax.random.fold_in(key_of[13], 71), 0)
    item_factors = jnp.clip(-0.125 + 0.375 * jax.random.uniform(key_of[9], (NI, R), jnp.float32) ** steps_of(key_of[9], (NI, R), ((0, 128),), -0.2, 0.2), -0.125, 0.25).astype(jnp.bfloat16)
    context_factors = jnp.clip(jax.random.uniform(key_of[10], (CTX, R), jnp.float32, -0.125, 0.25), -0.125, 0.25).astype(jnp.bfloat16)
    profile = centred(key_of[11], (USERS, FEAT), 32.0, 192.0, ((0, 128), (1, 4)))
    feature_factors = centred(key_of[12], (FEAT, R), 1.0, 6.0, ((0, 4),))
    return {"tile_users": tile_users, "tile_owners": tile_owners, "tile_blocks": tile_blocks, "tile_contexts": tile_contexts, "row_users": row_users, "row_items": row_items, "row_contexts": row_contexts, "tile_values": tile_values, "tile_count": tile_count, "item_factors": item_factors, "context_factors": context_factors, "profile": profile, "feature_factors": feature_factors}


RIDGE = 1.0

def gram(matrix):
    return lax.dot_general(matrix.astype(jnp.float32), matrix.astype(jnp.float32), (((0,), (0,)), ((), ())), preferred_element_type=jnp.float32)

def solve_rows(normal, right_side):
    cholesky_factor = jnp.linalg.cholesky(normal)
    return jax.scipy.linalg.cho_solve((cholesky_factor, True), right_side.T).T

def reference(tile_users, tile_owners, tile_blocks, tile_contexts, row_users, row_items, row_contexts, tile_values, tile_count, item_factors, context_factors, profile, feature_factors):
    devices_all = N_USERS * N_ITEMS

    def per_device(pieces):
        t_users, t_owners, t_blocks, t_ctx, r_users, r_items, r_ctx, values, live_count = pieces
        alive = (jnp.arange(TILES_DEV, dtype=jnp.int32) < live_count).astype(jnp.float32)
        users_local = t_users[:, None] * UB + r_users
        items_global = (t_owners[:, 0] * BLK_OWN + t_blocks)[:, None] * IB + r_items
        ctx_global = t_ctx[:, None] * CB + r_ctx
        weighted = values.astype(jnp.float32) * alive[:, None]
        row_terms = weighted[:, :, None] * item_factors[items_global].astype(jnp.float32) * context_factors[ctx_global].astype(jnp.float32)
        return jax.ops.segment_sum(row_terms.reshape(-1, R), users_local.reshape(-1).astype(jnp.int32), num_segments=U_DEV)
    pieces = (tile_users.reshape(devices_all, TILES_DEV), tile_owners.reshape(devices_all, TILES_DEV, 1), tile_blocks.reshape(devices_all, TILES_DEV), tile_contexts.reshape(devices_all, TILES_DEV), row_users.reshape(devices_all, TILES_DEV, TR), row_items.reshape(devices_all, TILES_DEV, TR), row_contexts.reshape(devices_all, TILES_DEV, TR), tile_values.reshape(devices_all, TILES_DEV, TR), tile_count.reshape(devices_all))
    partial_terms = lax.map(per_device, pieces)
    mttkrp = jnp.sum(partial_terms.reshape(N_USERS, N_ITEMS, U_DEV, R), axis=1).reshape(USERS, R)
    right_side = mttkrp + jnp.dot(profile.astype(jnp.float32), feature_factors.astype(jnp.float32), preferred_element_type=jnp.float32)
    identity = jnp.eye(R, dtype=jnp.float32)
    normal = gram(item_factors) * gram(context_factors) + gram(feature_factors) + RIDGE * identity
    user_factors = solve_rows(normal, right_side).astype(jnp.bfloat16)
    user_gram = gram(user_factors) + RIDGE * identity
    feature_right = lax.dot_general(profile.astype(jnp.float32), user_factors.astype(jnp.float32), (((0,), (0,)), ((), ())), preferred_element_type=jnp.float32)
    feature_new = solve_rows(user_gram, feature_right).astype(jnp.bfloat16)
    return (user_factors, feature_new)
```

```python
import functools

import jax
import jax.numpy as jnp
from jax import lax
from jax.experimental import pallas as pl
from jax.experimental.pallas import tpu as pltpu
from jax.sharding import PartitionSpec as P

NZ, NX, NC, NY = 16, 4, 2, 4
R = 256
CB, IB, UB, TR = 128, 16, 16, 128
TILES = 128
SLAB = 2048
RIDGE = 1.0
MESH = pl.DeviceIdType.MESH
F32 = jnp.float32
BF16 = jnp.bfloat16
HIGHEST = lax.Precision.HIGHEST
VMEM_LIMIT = 56 * 1024 * 1024


def position():
    u = lax.axis_index("users")
    y = lax.axis_index("items")
    return lax.div(u, 8), lax.rem(lax.div(u, 2), 4), lax.rem(u, 2), y


def neighbour(dz=0, dx=0, dc=0, dy=0):
    z, x, c, y = position()
    zz = lax.rem(z + dz + NZ, NZ)
    xx = lax.rem(x + dx + NX, NX)
    cc = lax.rem(c + dc, NC)
    return (zz * 8 + xx * 2 + cc, lax.rem(y + dy + NY, NY))


def greet(devices):
    barrier = pltpu.get_barrier_semaphore()
    for device in devices:
        pl.semaphore_signal(barrier, inc=1, device_id=device, device_id_type=MESH)
    pl.semaphore_wait(barrier, len(devices))


class Sender:
    def __init__(self, send_sem, recv_sem):
        self.send_sem, self.recv_sem, self.sent = send_sem, recv_sem, []

    def __call__(self, src, dst, device):
        i = len(self.sent)
        copy = pltpu.make_async_remote_copy(
            src_ref=src,
            dst_ref=dst,
            send_sem=self.send_sem.at[i],
            recv_sem=self.recv_sem.at[i],
            device_id=device,
            device_id_type=MESH,
        )
        copy.start()
        self.sent.append(copy)
        return copy

    def finish(self):
        for copy in self.sent:
            copy.wait_send()


def gather_kernel(item_ref, feat_ref, tab, fall, send_sem, recv_sem):
    c = position()[2]
    xp, xm, x2 = neighbour(dx=1), neighbour(dx=-1), neighbour(dx=2)
    zp, zm, sib = neighbour(dz=1), neighbour(dz=-1), neighbour(dc=1)
    yp, ym, y2 = neighbour(dy=1), neighbour(dy=-1), neighbour(dy=2)
    tab[0, 0, 0, 0] = item_ref[0:32, :]
    tab[1, 0, 0, 0] = item_ref[32:64, :]
    greet([xp, xm, x2, zp, zm, sib, yp, ym, y2])
    go = Sender(send_sem, recv_sem)

    own = tab.at[0, 0, 0, 0]
    first = [go(own, tab.at[0, 0, 0, 3], xp), go(own, tab.at[0, 0, 0, 1], xm), go(own, tab.at[0, 0, 0, 2], x2)]

    def ring1(s):
        if s < 7:
            return (
                go(tab.at[1, 0, (-s) % 16, 0], tab.at[1, 0, (-s - 1) % 16, 0], zp),
                go(tab.at[1, 0, s, 0], tab.at[1, 0, s + 1, 0], zm),
            )
        return (
            go(tab.at[1, 0, 9, 0, pl.ds(0, 16)], tab.at[1, 0, 8, 0, pl.ds(0, 16)], zp),
            go(tab.at[1, 0, 7, 0, pl.ds(16, 16)], tab.at[1, 0, 8, 0, pl.ds(16, 16)], zm),
        )

    def ring0(s):
        if s < 7:
            return (
                go(tab.at[0, 0, (-s) % 16], tab.at[0, 0, (-s - 1) % 16], zp),
                go(tab.at[0, 0, s], tab.at[0, 0, s + 1], zm),
            )
        return (
            go(tab.at[0, 0, 9, pl.ds(0, 2)], tab.at[0, 0, 8, pl.ds(0, 2)], zp),
            go(tab.at[0, 0, 7, pl.ds(2, 2)], tab.at[0, 0, 8, pl.ds(2, 2)], zm),
        )

    def cross(lo, n):
        return (
            lo,
            n,
            go(tab.at[1, 0, pl.ds(lo, n), 0], tab.at[1, 0, pl.ds(lo, n), 3], xp),
            go(tab.at[1, 0, pl.ds(lo, n), 0], tab.at[1, 0, pl.ds(lo, n), 1], xm),
        )

    def cross_on(group):
        lo, n, p, m = group
        d = pl.ds(lo, n)
        p.wait_recv()
        a = go(tab.at[1, 0, d, 3, pl.ds(0, 16)], tab.at[1, 0, d, 2, pl.ds(0, 16)], xp)
        m.wait_recv()
        b = go(tab.at[1, 0, d, 1, pl.ds(16, 16)], tab.at[1, 0, d, 2, pl.ds(16, 16)], xm)
        return (lo, n, a, b)

    def share(half, lo, n):
        return go(tab.at[half, 0, pl.ds(lo, n)], tab.at[half, 1, pl.ds(lo, n)], sib)

    shared = []

    def cross_off(group):
        lo, n, a, b = group
        a.wait_recv()
        b.wait_recv()
        shared.append(share(1, lo, n))

    r1 = ring1(0)
    crossing, crossed = [cross(0, 1)], []
    rows = pl.ds(pl.multiple_of(c * 256, 256), 256)
    feats = [
        go(feat_ref.at[rows], fall.at[0, 2], yp),
        go(feat_ref.at[rows], fall.at[0, 0], ym),
        go(feat_ref.at[rows], fall.at[0, 1], y2),
    ]
    for copy in first:
        copy.wait_recv()
    r0 = ring0(0)
    shared.append(share(0, 0, 1))
    for s in range(8):
        for copy in r1:
            copy.wait_recv()
        if s < 7:
            r1 = ring1(s + 1)
        for copy in r0:
            copy.wait_recv()
        if s < 7:
            r0 = ring0(s + 1)
        for group in crossed:
            cross_off(group)
        crossed = [cross_on(group) for group in crossing]
        crossing = []
        if s % 2 == 1:
            for lo, n in ((s, 2), (15 - s, 2)) if s < 7 else ((7, 2), (9, 1)):
                crossing.append(cross(lo, n))
                shared.append(share(0, lo, n))
        if s == 6:
            for copy in feats:
                copy.wait_recv()
            shared.append(go(fall.at[0], fall.at[1], sib))
    for group in crossed:
        cross_off(group)
    for group in crossing:
        cross_off(cross_on(group))
    for copy in shared:
        copy.wait_recv()
    go.finish()


def tile_kernel(item_at, context_at, user_at, tab, contexts, keys, users, values, profile, features, out):
    for i in range(SLAB // 256):
        rows = pl.ds(i * 256, 256)
        out[rows, :] = jnp.dot(profile[rows, :], features[...], preferred_element_type=F32)
    lane128 = lax.broadcasted_iota(jnp.int32, (TR, CB), 1)
    lane16 = lax.broadcasted_iota(jnp.int32, (TR, IB), 1)
    sub16 = lax.broadcasted_iota(jnp.int32, (UB, TR), 0)
    group = 8

    def step(g, carry):
        key = keys[g]
        user = users[pl.ds(pl.multiple_of(g * group, group), group), :]
        value = values[pl.ds(pl.multiple_of(g * group, group), group), :]
        sums = []
        for t in range(group):
            k = key[:, t : t + 1]
            context_onehot = (lax.shift_right_logical(jnp.broadcast_to(k, (TR, CB)), 4) == lane128).astype(F32).astype(BF16)
            item_onehot = (jnp.bitwise_and(jnp.broadcast_to(k, (TR, IB)), 15) == lane16).astype(F32).astype(BF16)
            at = g * group + t
            context_rows = contexts[pl.ds(pl.multiple_of(context_at[at], CB), CB), :]
            item_rows = tab[pl.ds(pl.multiple_of(item_at[at], IB), IB), :]
            product = jnp.dot(context_onehot, context_rows, preferred_element_type=F32) * jnp.dot(
                item_onehot, item_rows, preferred_element_type=F32
            )
            high = product.astype(BF16)
            low = (product - high.astype(F32)).astype(BF16)
            weight = jnp.where(user[t : t + 1, :] == sub16, value[t : t + 1, :], 0.0).astype(BF16)
            sums.append(
                jnp.dot(weight, high, preferred_element_type=F32) + jnp.dot(weight, low, preferred_element_type=F32)
            )
        for t in range(group):
            rows = pl.ds(pl.multiple_of(user_at[g * group + t], UB), UB)
            out[rows, :] += sums[t]
        return carry

    lax.fori_loop(0, TILES // group, step, 0)


def inverse(a, size=R, panel=32):
    lane = lax.broadcasted_iota(jnp.int32, (panel, size), 1)
    sub = lax.broadcasted_iota(jnp.int32, (panel, size), 0)
    wide = lax.broadcasted_iota(jnp.int32, (size, size), 1)
    for p in range(size // panel):
        lo = p * panel
        block = a[lo : lo + panel, :]
        for k in range(panel):
            at = lo + k
            column = jnp.broadcast_to(block[:, at : at + 1], (panel, size))
            pivot = 1.0 / jnp.broadcast_to(column[k : k + 1, :], (panel, size))
            row = jnp.where(lane == at, pivot, jnp.broadcast_to(block[k : k + 1, :], (panel, size)) * pivot)
            block = jnp.where(sub == k, row, jnp.where(lane == at, 0.0, block) - column * row)
        left = a[:, lo : lo + panel]
        a = jnp.where((wide >= lo) & (wide < lo + panel), 0.0, a) - jnp.dot(
            left, block, preferred_element_type=F32, precision=HIGHEST
        )
        pieces = [a[:lo, :]] if lo else []
        pieces.append(block)
        if lo + panel < size:
            pieces.append(a[lo + panel :, :])
        a = jnp.concatenate(pieces, axis=0)
    return a


def eye(size=R):
    return (
        lax.broadcasted_iota(jnp.int32, (size, size), 0) == lax.broadcasted_iota(jnp.int32, (size, size), 1)
    ).astype(F32)


def gram(a, b):
    return lax.dot_general(a, b, (((0,), (0,)), ((), ())), preferred_element_type=F32)


def normal_kernel(tab, contexts, features, fall, out):
    items = lax.fori_loop(
        0,
        8,
        lambda i, acc: acc + gram(tab[pl.ds(i * 1024, 1024), :], tab[pl.ds(i * 1024, 1024), :]),
        jnp.zeros((R, R), F32),
    )
    normal = items * gram(contexts[...], contexts[...]) + gram(features[...], features[...])
    normal = normal + gram(fall[...], fall[...]) + RIDGE * eye()
    out[...] = inverse(normal)


def user_kernel(part, inv, out, passing, landed, send_sem, recv_sem):
    y = position()[3]
    after, before = lax.rem(y + 1, NY), lax.rem(y + 3, NY)
    across = lax.rem(y + 2, NY)
    yp, ym = neighbour(dy=1), neighbour(dy=-1)
    top, low = pl.ds(0, 256), pl.ds(256, 256)
    greet([yp, ym])
    go = Sender(send_sem, recv_sem)
    ap = go(part.at[across, top], passing.at[0], yp)
    am = go(part.at[across, low], passing.at[1], ym)
    bp = go(part.at[after, low], landed.at[0], yp)
    bm = go(part.at[before, top], landed.at[1], ym)
    ap.wait_recv()
    passing[2] = passing[0] + part[after, top, :]
    cp = go(passing.at[2], landed.at[2], yp)
    am.wait_recv()
    passing[3] = passing[1] + part[before, low, :]
    cm = go(passing.at[3], landed.at[3], ym)
    bm.wait_recv()
    cp.wait_recv()
    total = part[y, top, :] + landed[1] + landed[2]
    out[y, top, :] = jnp.dot(total, inv[...], preferred_element_type=F32, precision=HIGHEST).astype(BF16)
    up0 = go(out.at[y, top], out.at[y, top], yp)
    um0 = go(out.at[y, top], out.at[y, top], ym)
    bp.wait_recv()
    cm.wait_recv()
    total = part[y, low, :] + landed[0] + landed[3]
    out[y, low, :] = jnp.dot(total, inv[...], preferred_element_type=F32, precision=HIGHEST).astype(BF16)
    up1 = go(out.at[y, low], out.at[y, low], yp)
    um1 = go(out.at[y, low], out.at[y, low], ym)
    up0.wait_recv()
    vp = go(out.at[before, top], out.at[before, top], yp)
    um1_wait = um1
    um0.wait_recv()
    um1_wait.wait_recv()
    vm = go(out.at[after, low], out.at[after, low], ym)
    up1.wait_recv()
    vp.wait_recv()
    vm.wait_recv()
    go.finish()


def reduce_kernel(uf, profile, outg, outf, pg, pf, cg, cf, sg, sf, xg, xf, tg, tf, zg, zf, send_sem, recv_sem):
    z, x, c, _ = position()
    sib = neighbour(dc=1)
    xs = [neighbour(dx=d) for d in range(1, NX)]
    zs = [neighbour(dz=d) for d in range(1, NZ)]
    whole = gram(uf[...], uf[...])
    pg[0] = whole[:, :128]
    pg[1] = whole[:, 128:]
    whole = gram(profile[...], uf[...])
    pf[0] = whole[:, :128]
    pf[1] = whole[:, 128:]
    greet([sib] + xs + zs)
    go = Sender(send_sem, recv_sem)
    other = lax.rem(c + 1, 2)
    kg = go(pg.at[other], cg, sib)
    kf = go(pf.at[other], cf, sib)

    def over_x(k, part, came, held, slots, rows):
        k.wait_recv()
        held[...] = (part[c] + came[...]).reshape(NX, rows, 128)
        return [go(held.at[lax.rem(x + d, NX)], slots.at[d - 1], xs[d - 1]) for d in range(1, NX)]

    ag = over_x(kg, pg, cg, sg, xg, 64)
    af = over_x(kf, pf, cf, sf, xf, 128)

    def over_z(copies, held, slots, split, zslots, rows):
        total = held[x]
        for d, copy in enumerate(copies):
            copy.wait_recv()
            total = total + slots[d]
        for i in range(NZ):
            split[i] = total[i * rows : (i + 1) * rows, :]
        return [go(split.at[lax.rem(z + d, NZ)], zslots.at[d - 1], zs[d - 1]) for d in range(1, NZ)]

    bg = over_z(ag, sg, xg, tg, zg, 4)
    bf = over_z(af, sf, xf, tf, zf, 8)

    def back_z(copies, split, zslots, out):
        total = split[z]
        for d, copy in enumerate(copies):
            copy.wait_recv()
            total = total + zslots[d]
        out[c, x, z] = total
        return [go(out.at[c, x, z], out.at[c, x, z], zs[d - 1]) for d in range(1, NZ)]

    hg = back_z(bg, tg, zg, outg)
    hf = back_z(bf, tf, zf, outf)

    def back_x(copies, out):
        for copy in copies:
            copy.wait_recv()
        return [go(out.at[c, x], out.at[c, x], xs[d - 1]) for d in range(1, NX)]

    ig = back_x(hg, outg)
    jf = back_x(hf, outf)

    def back_c(copies, out):
        for copy in copies:
            copy.wait_recv()
        return go(out.at[c], out.at[c], sib)

    lg = back_c(ig, outg)
    lf = back_c(jf, outf)
    lg.wait_recv()
    lf.wait_recv()
    go.finish()


def feature_kernel(gathered, right, out, normal):
    for h in range(2):
        for x in range(NX):
            for z in range(NZ):
                at = x * 64 + z * 4
                normal[at : at + 4, h * 128 : (h + 1) * 128] = gathered[h, x, z]
    inv = inverse(normal[...] + RIDGE * eye())
    total = jnp.dot(right[0], inv[:128, :], preferred_element_type=F32, precision=HIGHEST)
    total = total + jnp.dot(right[1], inv[128:, :], preferred_element_type=F32, precision=HIGHEST)
    out[...] = total.astype(BF16)


VM = pl.BlockSpec(memory_space=pltpu.VMEM)
SM = pl.BlockSpec(memory_space=pltpu.SMEM)


def remote_params(number):
    return pltpu.CompilerParams(collective_id=number, has_side_effects=True, vmem_limit_bytes=VMEM_LIMIT)


PLAIN = pltpu.CompilerParams(vmem_limit_bytes=VMEM_LIMIT)


def shape(dims, dtype):
    return jax.ShapeDtypeStruct(dims, dtype)


def sems(n):
    return [pltpu.SemaphoreType.DMA((n,)), pltpu.SemaphoreType.DMA((n,))]


def local(
    tile_users,
    tile_owners,
    tile_blocks,
    tile_contexts,
    row_users,
    row_items,
    row_contexts,
    tile_values,
    tile_count,
    item_factors,
    context_factors,
    profile,
    feature_factors,
):
    z, x, c, _ = position()
    owners = tile_owners.reshape(TILES)
    blocks = tile_blocks.reshape(TILES)
    rel_z = (owners // 8 - z) % NZ
    rel_x = (owners // 2 % 4 - x) % NX
    rel_c = (owners % 2 - c) % NC
    item_at = ((((blocks // 2) * 2 + rel_c) * NZ + rel_z) * NX + rel_x) * 32 + (blocks % 2) * IB
    context_at = tile_contexts.reshape(TILES) * CB
    user_at = tile_users.reshape(TILES) * UB
    keys = row_contexts.reshape(TILES, TR) * IB + row_items.reshape(TILES, TR)
    keys = keys.reshape(TILES // 8, 8, TR).transpose(0, 2, 1)
    alive = jnp.arange(TILES, dtype=jnp.int32) < tile_count.reshape(())
    values = jnp.where(alive[:, None], tile_values.reshape(TILES, TR).astype(F32), 0.0)
    users = row_users.reshape(TILES, TR)

    tab, fall = pl.pallas_call(
        gather_kernel,
        out_shape=(shape((2, 2, NZ, NX, 32, R), BF16), shape((2, 3, 256, R), BF16)),
        in_specs=[VM, VM],
        out_specs=(VM, VM),
        scratch_shapes=sems(96),
        compiler_params=remote_params(0),
        name="gather_items",
    )(item_factors, feature_factors)
    tab = tab.reshape(8192, R)
    fall = fall.reshape(1536, R)
    part = pl.pallas_call(
        tile_kernel,
        out_shape=shape((SLAB, R), F32),
        in_specs=[SM] * 3 + [VM] * 7,
        out_specs=VM,
        compiler_params=PLAIN,
        name="tiles",
    )(item_at, context_at, user_at, tab, context_factors, keys, users, values, profile, feature_factors)
    inv = pl.pallas_call(
        normal_kernel,
        out_shape=shape((R, R), F32),
        in_specs=[VM] * 4,
        out_specs=VM,
        compiler_params=PLAIN,
        name="normal_inverse",
    )(tab, context_factors, feature_factors, fall)
    uf = pl.pallas_call(
        user_kernel,
        out_shape=shape((NY, 512, R), BF16),
        in_specs=[VM, VM],
        out_specs=VM,
        scratch_shapes=[pltpu.VMEM((4, 256, R), F32), pltpu.VMEM((4, 256, R), F32)] + sems(12),
        compiler_params=remote_params(1),
        name="user_rows",
    )(part.reshape(NY, 512, R), inv)
    uf = uf.reshape(SLAB, R)
    gathered, right = pl.pallas_call(
        reduce_kernel,
        out_shape=(shape((2, NX, NZ, 4, 128), F32), shape((2, NX, NZ, 8, 128), F32)),
        in_specs=[VM, VM],
        out_specs=(VM, VM),
        scratch_shapes=[
            pltpu.VMEM((2, 256, 128), F32),
            pltpu.VMEM((2, 512, 128), F32),
            pltpu.VMEM((256, 128), F32),
            pltpu.VMEM((512, 128), F32),
            pltpu.VMEM((NX, 64, 128), F32),
            pltpu.VMEM((NX, 128, 128), F32),
            pltpu.VMEM((3, 64, 128), F32),
            pltpu.VMEM((3, 128, 128), F32),
            pltpu.VMEM((NZ, 4, 128), F32),
            pltpu.VMEM((NZ, 8, 128), F32),
            pltpu.VMEM((NZ - 1, 4, 128), F32),
            pltpu.VMEM((NZ - 1, 8, 128), F32),
        ]
        + sems(76),
        compiler_params=remote_params(2),
        name="sum_over_users",
    )(uf, profile)
    feature_new = pl.pallas_call(
        feature_kernel,
        out_shape=shape((512, R), BF16),
        in_specs=[VM, VM],
        out_specs=VM,
        scratch_shapes=[pltpu.VMEM((R, R), F32)],
        compiler_params=PLAIN,
        name="feature_rows",
    )(gathered, right.reshape(2, 512, 128))
    return (uf, feature_new)


def solution(mesh):
    in_specs = (
        P("users", "items", None),
        P("users", "items", None, None),
        P("users", "items", None),
        P("users", "items", None),
        P("users", "items", None, None),
        P("users", "items", None, None),
        P("users", "items", None, None),
        P("users", "items", None, None),
        P("users", "items"),
        P("users", None),
        P(),
        P("users", "items"),
        P("items", None),
    )
    out_specs = (P("users", None), P("items", None))
    return jax.shard_map(local, mesh=mesh, in_specs=in_specs, out_specs=out_specs, check_vma=False)
```

```python
import functools

import jax
import jax.numpy as jnp
from jax import lax
from jax.experimental import pallas as pl
from jax.experimental.pallas import tpu as pltpu
from jax.sharding import PartitionSpec as P

NZ, NX, NC, NY = 16, 4, 2, 4
R = 256
CB, IB, UB, TR = 128, 16, 16, 128
TILES = 128
SLAB = 2048
RIDGE = 1.0
MESH = pl.DeviceIdType.MESH
F32 = jnp.float32
BF16 = jnp.bfloat16
HIGHEST = lax.Precision.HIGHEST
VMEM_LIMIT = 56 * 1024 * 1024


def position():
    u = lax.axis_index("users")
    y = lax.axis_index("items")
    return lax.div(u, 8), lax.rem(lax.div(u, 2), 4), lax.rem(u, 2), y


def neighbour(dz=0, dx=0, dc=0, dy=0):
    z, x, c, y = position()
    zz = lax.rem(z + dz + NZ, NZ)
    xx = lax.rem(x + dx + NX, NX)
    cc = lax.rem(c + dc, NC)
    return (zz * 8 + xx * 2 + cc, lax.rem(y + dy + NY, NY))


def greet(devices):
    barrier = pltpu.get_barrier_semaphore()
    for device in devices:
        pl.semaphore_signal(barrier, inc=1, device_id=device, device_id_type=MESH)
    pl.semaphore_wait(barrier, len(devices))


class Sender:
    def __init__(self, send_sem, recv_sem):
        self.send_sem, self.recv_sem, self.sent = send_sem, recv_sem, []

    def __call__(self, src, dst, device):
        i = len(self.sent)
        copy = pltpu.make_async_remote_copy(
            src_ref=src,
            dst_ref=dst,
            send_sem=self.send_sem.at[i],
            recv_sem=self.recv_sem.at[i],
            device_id=device,
            device_id_type=MESH,
        )
        copy.start()
        self.sent.append(copy)
        return copy

    def finish(self):
        for copy in self.sent:
            copy.wait_send()


def gather_kernel(item_ref, feat_ref, tab, fall, send_sem, recv_sem):
    c = position()[2]
    xp, xm, x2 = neighbour(dx=1), neighbour(dx=-1), neighbour(dx=2)
    zp, zm, sib = neighbour(dz=1), neighbour(dz=-1), neighbour(dc=1)
    yp, ym, y2 = neighbour(dy=1), neighbour(dy=-1), neighbour(dy=2)
    tab[0, 0, 0] = item_ref[...]
    greet([xp, xm, x2, zp, zm, sib, yp, ym, y2])
    go = Sender(send_sem, recv_sem)

    def up(s, e):
        return go(tab.at[0, (-s) % 16, e], tab.at[0, (-s - 1) % 16, e], zp)

    def down(s, e):
        return go(tab.at[0, s, e], tab.at[0, s + 1, e], zm)

    def share(d):
        return go(tab.at[0, d], tab.at[1, d], sib)

    own = tab.at[0, 0, 0]
    arrivals = {
        3: go(own, tab.at[0, 0, 3], xp),
        1: go(own, tab.at[0, 0, 1], xm),
        2: go(own, tab.at[0, 0, 2], x2),
    }
    ups, downs = {0: up(0, 0)}, {0: down(0, 0)}
    rows = pl.ds(pl.multiple_of(c * 256, 256), 256)
    feats = [
        go(feat_ref.at[rows], fall.at[0, 2], yp),
        go(feat_ref.at[rows], fall.at[0, 0], ym),
        go(feat_ref.at[rows], fall.at[0, 1], y2),
    ]
    order = (0, 3, 1, 2)
    for e in order[1:]:
        arrivals[e].wait_recv()
        ups[e], downs[e] = up(0, e), down(0, e)
    shared = [share(0)]
    for s in range(8):
        for e in order:
            if e in ups:
                ups.pop(e).wait_recv()
                if s < 6 or (s == 6 and e in (0, 3)):
                    ups[e] = up(s + 1, e)
            if e in downs:
                downs.pop(e).wait_recv()
                if s < 6 or (s == 6 and e in (1, 2)):
                    downs[e] = down(s + 1, e)
        shared.append(share(s + 1))
        if s < 7:
            shared.append(share(15 - s))
        if s == 5:
            for copy in feats:
                copy.wait_recv()
            shared.append(go(fall.at[0], fall.at[1], sib))
    for copy in shared:
        copy.wait_recv()
    go.finish()


def tile_kernel(
    owners, blocks, tile_contexts, tile_users, count, tab, contexts, row_contexts, row_items, row_users, values, profile, features, out
):
    z, x, c, _ = position()
    live = count[0]
    for i in range(SLAB // 256):
        rows = pl.ds(i * 256, 256)
        out[rows, :] = jnp.dot(profile[rows, :], features[...], preferred_element_type=F32)
    lane128 = lax.broadcasted_iota(jnp.int32, (TR, CB), 1)
    lane16 = lax.broadcasted_iota(jnp.int32, (TR, IB), 1)
    sub16 = lax.broadcasted_iota(jnp.int32, (UB, TR), 0)
    group = 16

    def item_row(at):
        owner = owners[at]
        rel_z = jnp.bitwise_and(lax.shift_right_logical(owner, 3) - z + NZ, NZ - 1)
        rel_x = jnp.bitwise_and(lax.shift_right_logical(owner, 1) - x + NX, NX - 1)
        rel_c = jnp.bitwise_and(owner + c, 1)
        return ((rel_c * NZ + rel_z) * NX + rel_x) * 64 + blocks[at] * IB

    def step(g, carry):
        rows = pl.ds(pl.multiple_of(g * group, group), group)
        key = jnp.transpose(row_contexts[rows, :] * IB + row_items[rows, :])
        user = row_users[rows, :]
        value = values[rows, :].astype(F32)
        sums = []
        for t in range(group):
            k = key[:, t : t + 1]
            context_onehot = (lax.shift_right_logical(jnp.broadcast_to(k, (TR, CB)), 4) == lane128).astype(F32).astype(BF16)
            item_onehot = (jnp.bitwise_and(jnp.broadcast_to(k, (TR, IB)), 15) == lane16).astype(F32).astype(BF16)
            at = g * group + t
            context_rows = contexts[pl.ds(pl.multiple_of(tile_contexts[at] * CB, CB), CB), :]
            item_rows = tab[pl.ds(pl.multiple_of(item_row(at), IB), IB), :]
            product = jnp.dot(context_onehot, context_rows, preferred_element_type=F32) * jnp.dot(
                item_onehot, item_rows, preferred_element_type=F32
            )
            high = product.astype(BF16)
            low = (product - high.astype(F32)).astype(BF16)
            weight = jnp.where((user[t : t + 1, :] == sub16) & (at < live), value[t : t + 1, :], 0.0).astype(BF16)
            sums.append(
                jnp.dot(weight, high, preferred_element_type=F32) + jnp.dot(weight, low, preferred_element_type=F32)
            )
        for t in range(group):
            place = pl.ds(pl.multiple_of(tile_users[g * group + t] * UB, UB), UB)
            out[place, :] += sums[t]
        return carry

    lax.fori_loop(0, TILES // group, step, 0)


def sweep(block, group):
    panel, size = block.shape
    lane = lax.broadcasted_iota(jnp.int32, (panel, size), 1)
    lane1 = lax.broadcasted_iota(jnp.int32, (1, size), 1)
    sub = lax.broadcasted_iota(jnp.int32, (panel, size), 0)
    sub1 = lax.broadcasted_iota(jnp.int32, (panel, 128), 0)

    def wide(v):
        return jnp.concatenate([v] * (size // 128), axis=1)

    for base in range(0, panel, group):
        columns = [jnp.broadcast_to(block[:, base + j : base + j + 1], (panel, 128)) for j in range(group)]
        for k in range(group):
            at = base + k
            pivot = 1.0 / columns[k][at : at + 1, :]
            row = jnp.where(lane1 == at, wide(pivot), block[at : at + 1, :] * wide(pivot))
            block = jnp.where(sub == at, row, jnp.where(lane == at, 0.0, block) - wide(columns[k]) * row)
            for j in range(k + 1, group):
                factor = columns[j][at : at + 1, :] * pivot
                columns[j] = jnp.where(sub1 == at, factor, columns[j] - columns[k] * factor)
    return block


def invert(ref, between=(), size=R, panel=32, group=16):
    hooks = dict(between)
    lane = lax.broadcasted_iota(jnp.int32, (size - panel, size), 1)

    def step(p, carry):
        block = sweep(ref[0:panel, :], group)
        rest = ref[panel:, :]
        update = jnp.dot(rest[:, 0:panel], block, preferred_element_type=F32, precision=HIGHEST)
        ref[0 : size - panel, :] = pltpu.roll(jnp.where(lane < panel, 0.0, rest) - update, size - panel, 1)
        ref[size - panel :, :] = pltpu.roll(block, size - panel, 1)
        return carry

    done = 0
    for p in sorted(set(hooks) | {size // panel - 1}):
        lax.fori_loop(done, p + 1, step, 0)
        done = p + 1
        if p in hooks:
            hooks[p]()


def eye(size=R):
    return (
        lax.broadcasted_iota(jnp.int32, (size, size), 0) == lax.broadcasted_iota(jnp.int32, (size, size), 1)
    ).astype(F32)


def gram(a, b):
    return lax.dot_general(a, b, (((0,), (0,)), ((), ())), preferred_element_type=F32)


def user_kernel(part, tab, contexts, features, fall, out, inv, passing, landed, send_sem, recv_sem):
    y = position()[3]
    after, before = lax.rem(y + 1, NY), lax.rem(y + 3, NY)
    across = lax.rem(y + 2, NY)
    yp, ym = neighbour(dy=1), neighbour(dy=-1)
    top, low = pl.ds(0, 256), pl.ds(256, 256)
    greet([yp, ym])
    go = Sender(send_sem, recv_sem)
    ap = go(part.at[across, top], passing.at[0], yp)
    am = go(part.at[across, low], passing.at[1], ym)
    bp = go(part.at[after, low], landed.at[0], yp)
    bm = go(part.at[before, top], landed.at[1], ym)
    items = lax.fori_loop(
        0,
        8,
        lambda i, acc: acc + gram(tab[pl.ds(i * 1024, 1024), :], tab[pl.ds(i * 1024, 1024), :]),
        jnp.zeros((R, R), F32),
    )
    normal = items * gram(contexts[...], contexts[...]) + gram(features[...], features[...])
    inv[...] = normal + gram(fall[...], fall[...]) + RIDGE * eye()
    ap.wait_recv()
    passing[2] = passing[0] + part[after, top, :]
    cp = go(passing.at[2], landed.at[2], yp)
    am.wait_recv()
    passing[3] = passing[1] + part[before, low, :]
    cm = go(passing.at[3], landed.at[3], ym)
    invert(inv)
    bm.wait_recv()
    cp.wait_recv()
    total = part[y, top, :] + landed[1] + landed[2]
    out[y, top, :] = jnp.dot(total, inv[...], preferred_element_type=F32, precision=HIGHEST).astype(BF16)
    up0 = go(out.at[y, top], out.at[y, top], yp)
    um0 = go(out.at[y, top], out.at[y, top], ym)
    bp.wait_recv()
    cm.wait_recv()
    total = part[y, low, :] + landed[0] + landed[3]
    out[y, low, :] = jnp.dot(total, inv[...], preferred_element_type=F32, precision=HIGHEST).astype(BF16)
    um1 = go(out.at[y, low], out.at[y, low], ym)
    up1 = go(out.at[y, low], out.at[y, low], yp)
    up0.wait_recv()
    vp = go(out.at[before, top], out.at[before, top], yp)
    um0.wait_recv()
    um1.wait_recv()
    vm = go(out.at[after, low], out.at[after, low], ym)
    up1.wait_recv()
    vp.wait_recv()
    vm.wait_recv()
    go.finish()


def reduce_kernel(uf, profile, out, normal, outg, outf, pg, pf, cg, cf, sg, sf, xg, xf, tg, tf, zg, zf, send_sem, recv_sem):
    z, x, c, _ = position()
    sib = neighbour(dc=1)
    xs = [neighbour(dx=d) for d in range(1, NX)]
    zs = [neighbour(dz=d) for d in range(1, NZ)]
    greet([sib] + xs + zs)
    go = Sender(send_sem, recv_sem)
    other = lax.rem(c + 1, 2)
    whole = gram(uf[...], uf[...])
    pg[0] = whole[:, :128]
    pg[1] = whole[:, 128:]
    kg = go(pg.at[other], cg, sib)
    whole = gram(profile[...], uf[...])
    pf[0] = whole[:, :128]
    pf[1] = whole[:, 128:]
    kf = go(pf.at[other], cf, sib)

    def over_x(k, part, came, held, slots, rows):
        k.wait_recv()
        held[...] = (part[c] + came[...]).reshape(NX, rows, 128)
        return [go(held.at[lax.rem(x + d, NX)], slots.at[d - 1], xs[d - 1]) for d in range(1, NX)]

    ag = over_x(kg, pg, cg, sg, xg, 64)

    def over_z(copies, held, slots, split, zslots, rows):
        total = held[x]
        for d, copy in enumerate(copies):
            copy.wait_recv()
            total = total + slots[d]
        for i in range(NZ):
            split[i] = total[i * rows : (i + 1) * rows, :]
        return [go(split.at[lax.rem(z + d, NZ)], zslots.at[d - 1], zs[d - 1]) for d in range(1, NZ)]

    bg = over_z(ag, sg, xg, tg, zg, 4)
    af = over_x(kf, pf, cf, sf, xf, 128)

    def back_z(copies, split, zslots, out):
        total = split[z]
        for d, copy in enumerate(copies):
            copy.wait_recv()
            total = total + zslots[d]
        out[c, x, z] = total
        return [go(out.at[c, x, z], out.at[c, x, z], zs[d - 1]) for d in range(1, NZ)]

    hg = back_z(bg, tg, zg, outg)

    def back_x(copies, out):
        for copy in copies:
            copy.wait_recv()
        return [go(out.at[c, x], out.at[c, x], xs[d - 1]) for d in range(1, NX)]

    ig = back_x(hg, outg)
    bf = over_z(af, sf, xf, tf, zf, 8)

    def back_c(copies, out):
        for copy in copies:
            copy.wait_recv()
        return go(out.at[c], out.at[c], sib)

    back_c(ig, outg).wait_recv()
    for half in range(2):
        for i in range(NX):
            for j in range(NZ):
                at = i * 64 + j * 4
                normal[at : at + 4, half * 128 : (half + 1) * 128] = outg[half, i, j]
    normal[...] += RIDGE * eye()
    later = {}

    def third():
        later["z"] = back_z(bf, tf, zf, outf)

    def fourth():
        later["x"] = back_x(later["z"], outf)

    def fifth():
        later["c"] = back_c(later["x"], outf)

    invert(normal, ((1, third), (3, fourth), (5, fifth)))
    later["c"].wait_recv()
    total = jnp.dot(outf[0].reshape(512, 128), normal[0:128, :], preferred_element_type=F32, precision=HIGHEST)
    total = total + jnp.dot(outf[1].reshape(512, 128), normal[128:, :], preferred_element_type=F32, precision=HIGHEST)
    out[...] = total.astype(BF16)
    go.finish()


VM = pl.BlockSpec(memory_space=pltpu.VMEM)
SM = pl.BlockSpec(memory_space=pltpu.SMEM)


def remote_params(number):
    return pltpu.CompilerParams(collective_id=number, has_side_effects=True, vmem_limit_bytes=VMEM_LIMIT)


PLAIN = pltpu.CompilerParams(vmem_limit_bytes=VMEM_LIMIT)


def shape(dims, dtype):
    return jax.ShapeDtypeStruct(dims, dtype)


def sems(n):
    return [pltpu.SemaphoreType.DMA((n,)), pltpu.SemaphoreType.DMA((n,))]


def local(
    tile_users,
    tile_owners,
    tile_blocks,
    tile_contexts,
    row_users,
    row_items,
    row_contexts,
    tile_values,
    tile_count,
    item_factors,
    context_factors,
    profile,
    feature_factors,
):
    tab, fall = pl.pallas_call(
        gather_kernel,
        out_shape=(shape((2, NZ, NX, 64, R), BF16), shape((2, 3, 256, R), BF16)),
        in_specs=[VM, VM],
        out_specs=(VM, VM),
        scratch_shapes=sems(96),
        compiler_params=remote_params(0),
        name="gather_items",
    )(item_factors, feature_factors)
    tab = tab.reshape(8192, R)
    fall = fall.reshape(1536, R)
    part = pl.pallas_call(
        tile_kernel,
        out_shape=shape((SLAB, R), F32),
        in_specs=[SM] * 5 + [VM] * 8,
        out_specs=VM,
        compiler_params=PLAIN,
        name="tiles",
    )(
        tile_owners.reshape(TILES),
        tile_blocks.reshape(TILES),
        tile_contexts.reshape(TILES),
        tile_users.reshape(TILES),
        tile_count.reshape(1),
        tab,
        context_factors,
        row_contexts.reshape(TILES, TR),
        row_items.reshape(TILES, TR),
        row_users.reshape(TILES, TR),
        tile_values.reshape(TILES, TR),
        profile,
        feature_factors,
    )
    uf = pl.pallas_call(
        user_kernel,
        out_shape=shape((NY, 512, R), BF16),
        in_specs=[VM] * 5,
        out_specs=VM,
        scratch_shapes=[
            pltpu.VMEM((R, R), F32),
            pltpu.VMEM((4, 256, R), F32),
            pltpu.VMEM((4, 256, R), F32),
        ]
        + sems(12),
        compiler_params=remote_params(1),
        name="user_rows",
    )(part.reshape(NY, 512, R), tab, context_factors, feature_factors, fall)
    uf = uf.reshape(SLAB, R)
    feature_new = pl.pallas_call(
        reduce_kernel,
        out_shape=shape((512, R), BF16),
        in_specs=[VM, VM],
        out_specs=VM,
        scratch_shapes=[
            pltpu.VMEM((R, R), F32),
            pltpu.VMEM((2, NX, NZ, 4, 128), F32),
            pltpu.VMEM((2, NX, NZ, 8, 128), F32),
            pltpu.VMEM((2, 256, 128), F32),
            pltpu.VMEM((2, 512, 128), F32),
            pltpu.VMEM((256, 128), F32),
            pltpu.VMEM((512, 128), F32),
            pltpu.VMEM((NX, 64, 128), F32),
            pltpu.VMEM((NX, 128, 128), F32),
            pltpu.VMEM((3, 64, 128), F32),
            pltpu.VMEM((3, 128, 128), F32),
            pltpu.VMEM((NZ, 4, 128), F32),
            pltpu.VMEM((NZ, 8, 128), F32),
            pltpu.VMEM((NZ - 1, 4, 128), F32),
            pltpu.VMEM((NZ - 1, 8, 128), F32),
        ]
        + sems(76),
        compiler_params=remote_params(2),
        name="feature_rows",
    )(uf, profile)
    return (uf, feature_new)


def solution(mesh):
    in_specs = (
        P("users", "items", None),
        P("users", "items", None, None),
        P("users", "items", None),
        P("users", "items", None),
        P("users", "items", None, None),
        P("users", "items", None, None),
        P("users", "items", None, None),
        P("users", "items", None, None),
        P("users", "items"),
        P("users", None),
        P(),
        P("users", "items"),
        P("items", None),
    )
    out_specs = (P("users", None), P("items", None))
    return jax.shard_map(local, mesh=mesh, in_specs=in_specs, out_specs=out_specs, check_vma=False)
```

```python
import functools

import jax
import jax.numpy as jnp
from jax import lax
from jax.experimental import pallas as pl
from jax.experimental.pallas import tpu as pltpu
from jax.sharding import PartitionSpec as P

NZ, NX, NC, NY = 16, 4, 2, 4
R = 256
CB, IB, UB, TR = 128, 16, 16, 128
TILES = 128
SLAB = 2048
RIDGE = 1.0
MESH = pl.DeviceIdType.MESH
F32 = jnp.float32
BF16 = jnp.bfloat16
HIGHEST = lax.Precision.HIGHEST
VMEM_LIMIT = 56 * 1024 * 1024


def position():
    u = lax.axis_index("users")
    y = lax.axis_index("items")
    return lax.div(u, 8), lax.rem(lax.div(u, 2), 4), lax.rem(u, 2), y


def neighbour(dz=0, dx=0, dc=0, dy=0):
    z, x, c, y = position()
    zz = lax.rem(z + dz + NZ, NZ)
    xx = lax.rem(x + dx + NX, NX)
    cc = lax.rem(c + dc, NC)
    return (zz * 8 + xx * 2 + cc, lax.rem(y + dy + NY, NY))


def greet(devices):
    barrier = pltpu.get_barrier_semaphore()
    for device in devices:
        pl.semaphore_signal(barrier, inc=1, device_id=device, device_id_type=MESH)
    return lambda: pl.semaphore_wait(barrier, len(devices))


class Sender:
    def __init__(self, send_sem, recv_sem):
        self.send_sem, self.recv_sem, self.sent = send_sem, recv_sem, []

    def __call__(self, src, dst, device):
        i = len(self.sent)
        copy = pltpu.make_async_remote_copy(
            src_ref=src,
            dst_ref=dst,
            send_sem=self.send_sem.at[i],
            recv_sem=self.recv_sem.at[i],
            device_id=device,
            device_id_type=MESH,
        )
        copy.start()
        self.sent.append(copy)
        return copy

    def finish(self):
        for copy in self.sent:
            copy.wait_send()


def gather_kernel(item_ref, feat_ref, tab, fall, send_sem, recv_sem):
    c = position()[2]
    xp, xm, x2 = neighbour(dx=1), neighbour(dx=-1), neighbour(dx=2)
    zp, zm, sib = neighbour(dz=1), neighbour(dz=-1), neighbour(dc=1)
    yp, ym, y2 = neighbour(dy=1), neighbour(dy=-1), neighbour(dy=2)
    tab[0, 0, 0] = item_ref[...]
    greet([xp, xm, x2, zp, zm, sib, yp, ym, y2])()
    go = Sender(send_sem, recv_sem)

    def up(s, e):
        return go(tab.at[0, (-s) % 16, e], tab.at[0, (-s - 1) % 16, e], zp)

    def down(s, e):
        return go(tab.at[0, s, e], tab.at[0, s + 1, e], zm)

    def share(d):
        return go(tab.at[0, d], tab.at[1, d], sib)

    own = tab.at[0, 0, 0]
    arrivals = {
        3: go(own, tab.at[0, 0, 3], xp),
        1: go(own, tab.at[0, 0, 1], xm),
        2: go(own, tab.at[0, 0, 2], x2),
    }
    ups, downs = {0: up(0, 0)}, {0: down(0, 0)}
    rows = pl.ds(pl.multiple_of(c * 256, 256), 256)
    feats = [
        go(feat_ref.at[rows], fall.at[0, 2], yp),
        go(feat_ref.at[rows], fall.at[0, 0], ym),
        go(feat_ref.at[rows], fall.at[0, 1], y2),
    ]
    order = (0, 3, 1, 2)
    for e in order[1:]:
        arrivals[e].wait_recv()
        ups[e], downs[e] = up(0, e), down(0, e)
    shared = [share(0)]
    for s in range(8):
        for e in order:
            if e in ups:
                ups.pop(e).wait_recv()
                if s < 6 or (s == 6 and e in (0, 3)):
                    ups[e] = up(s + 1, e)
            if e in downs:
                downs.pop(e).wait_recv()
                if s < 6 or (s == 6 and e in (1, 2)):
                    downs[e] = down(s + 1, e)
        shared.append(share(s + 1))
        if s < 7:
            shared.append(share(15 - s))
        if s == 5:
            for copy in feats:
                copy.wait_recv()
            shared.append(go(fall.at[0], fall.at[1], sib))
    for copy in shared:
        copy.wait_recv()
    go.finish()


def item_row(owner, block, z, x, c):
    rel_z = jnp.bitwise_and(lax.shift_right_logical(owner, 3) - z + NZ, NZ - 1)
    rel_x = jnp.bitwise_and(lax.shift_right_logical(owner, 1) - x + NX, NX - 1)
    rel_c = jnp.bitwise_and(owner + c, 1)
    return ((rel_c * NZ + rel_z) * NX + rel_x) * 64 + block * IB


GROUP = 16


def tile_kernel(
    owners, blocks, tile_contexts, tile_users, count, tab, contexts, row_contexts, row_items, row_users, values, profile, features, out, high, low
):
    z, x, c, _ = position()
    live = count[0]
    for i in range(SLAB // 256):
        rows = pl.ds(i * 256, 256)
        out[rows, :] = jnp.dot(profile[rows, :], features[...], preferred_element_type=F32)
    lane128 = lax.broadcasted_iota(jnp.int32, (TR, CB), 1)
    lane16 = lax.broadcasted_iota(jnp.int32, (TR, IB), 1)
    sub16 = lax.broadcasted_iota(jnp.int32, (UB, TR), 0)

    def products(g, carry):
        rows = pl.ds(pl.multiple_of(g * GROUP, GROUP), GROUP)
        key = jnp.transpose(row_contexts[rows, :] * IB + row_items[rows, :])
        for t in range(GROUP):
            k = key[:, t : t + 1]
            context_onehot = (lax.shift_right_logical(jnp.broadcast_to(k, (TR, CB)), 4) == lane128).astype(F32).astype(BF16)
            item_onehot = (jnp.bitwise_and(jnp.broadcast_to(k, (TR, IB)), 15) == lane16).astype(F32).astype(BF16)
            at = g * GROUP + t
            context_rows = contexts[pl.ds(pl.multiple_of(tile_contexts[at] * CB, CB), CB), :]
            item_rows = tab[pl.ds(pl.multiple_of(item_row(owners[at], blocks[at], z, x, c), IB), IB), :]
            product = jnp.dot(context_onehot, context_rows, preferred_element_type=F32) * jnp.dot(
                item_onehot, item_rows, preferred_element_type=F32
            )
            top = product.astype(BF16)
            place = pl.ds(pl.multiple_of(at * TR, TR), TR)
            high[place, :] = top
            low[place, :] = (product - top.astype(F32)).astype(BF16)
        return carry

    def sums(g, carry):
        rows = pl.ds(pl.multiple_of(g * GROUP, GROUP), GROUP)
        user = row_users[rows, :]
        value = values[rows, :].astype(F32)
        done = []
        for t in range(GROUP):
            at = g * GROUP + t
            weight = jnp.where((user[t : t + 1, :] == sub16) & (at < live), value[t : t + 1, :], 0.0).astype(BF16)
            place = pl.ds(pl.multiple_of(at * TR, TR), TR)
            done.append(
                jnp.dot(weight, high[place, :], preferred_element_type=F32)
                + jnp.dot(weight, low[place, :], preferred_element_type=F32)
            )
        for t in range(GROUP):
            place = pl.ds(pl.multiple_of(tile_users[g * GROUP + t] * UB, UB), UB)
            out[place, :] += done[t]
        return carry

    lax.fori_loop(0, TILES // GROUP, products, 0)
    lax.fori_loop(0, TILES // GROUP, sums, 0)


def sweep(block, group):
    panel, size = block.shape
    lane = lax.broadcasted_iota(jnp.int32, (panel, size), 1)
    lane1 = lax.broadcasted_iota(jnp.int32, (1, size), 1)
    sub = lax.broadcasted_iota(jnp.int32, (panel, size), 0)
    sub1 = lax.broadcasted_iota(jnp.int32, (panel, 128), 0)

    def wide(v):
        return jnp.concatenate([v] * (size // 128), axis=1)

    for base in range(0, panel, group):
        columns = [jnp.broadcast_to(block[:, base + j : base + j + 1], (panel, 128)) for j in range(group)]
        for k in range(group):
            at = base + k
            pivot = 1.0 / columns[k][at : at + 1, :]
            row = jnp.where(lane1 == at, wide(pivot), block[at : at + 1, :] * wide(pivot))
            block = jnp.where(sub == at, row, jnp.where(lane == at, 0.0, block) - wide(columns[k]) * row)
            for j in range(k + 1, group):
                factor = columns[j][at : at + 1, :] * pivot
                columns[j] = jnp.where(sub1 == at, factor, columns[j] - columns[k] * factor)
    return block


def invert(ref, between=(), size=R, panel=32, group=16):
    hooks = dict(between)
    lane = lax.broadcasted_iota(jnp.int32, (size - panel, size), 1)

    def step(p, carry):
        block = sweep(ref[0:panel, :], group)
        rest = ref[panel:, :]
        update = jnp.dot(rest[:, 0:panel], block, preferred_element_type=F32, precision=HIGHEST)
        ref[0 : size - panel, :] = pltpu.roll(jnp.where(lane < panel, 0.0, rest) - update, size - panel, 1)
        ref[size - panel :, :] = pltpu.roll(block, size - panel, 1)
        return carry

    done = 0
    for p in sorted(set(hooks) | {size // panel - 1}):
        lax.fori_loop(done, p + 1, step, 0)
        done = p + 1
        if p in hooks:
            hooks[p]()


def eye(size=R):
    return (
        lax.broadcasted_iota(jnp.int32, (size, size), 0) == lax.broadcasted_iota(jnp.int32, (size, size), 1)
    ).astype(F32)


def gram(a, b):
    return lax.dot_general(a, b, (((0,), (0,)), ((), ())), preferred_element_type=F32)


def factor_kernel(
    part, tab, contexts, features, fall, profile, out, new,
    inv, passing, landed, outg, outf, pg, pf, cg, cf, sg, sf, xg, xf, tg, tf, zg, zf, yg, send_sem, recv_sem,
):
    z, x, c, y = position()
    after, before, across = lax.rem(y + 1, NY), lax.rem(y + 3, NY), lax.rem(y + 2, NY)
    yp, ym, y2 = neighbour(dy=1), neighbour(dy=-1), neighbour(dy=2)
    sib = neighbour(dc=1)
    xs = [neighbour(dx=d) for d in range(1, NX)]
    zs = [neighbour(dz=d) for d in range(1, NZ)]
    other = lax.rem(c + 1, 2)
    top, low = pl.ds(0, 256), pl.ds(256, 256)
    barrier = greet([yp, ym, y2, sib] + xs + zs)
    items = lax.fori_loop(
        0,
        8,
        lambda i, acc: acc + gram(tab[pl.ds(i * 1024, 1024), :], tab[pl.ds(i * 1024, 1024), :]),
        jnp.zeros((R, R), F32),
    )
    normal = items * gram(contexts[...], contexts[...]) + gram(features[...], features[...])
    inv[...] = normal + gram(fall[...], fall[...]) + RIDGE * eye()
    barrier()
    go = Sender(send_sem, recv_sem)

    def relay_up():
        ap.wait_recv()
        passing[2] = passing[0] + part[after, top, :]
        later["cp"] = go(passing.at[2], landed.at[2], yp)
        am.wait_recv()
        passing[3] = passing[1] + part[before, low, :]
        later["cm"] = go(passing.at[3], landed.at[3], ym)

    later = {}
    ap = go(part.at[across, top], passing.at[0], yp)
    am = go(part.at[across, low], passing.at[1], ym)
    bp = go(part.at[after, low], landed.at[0], yp)
    bm = go(part.at[before, top], landed.at[1], ym)
    invert(inv, ((3, relay_up),))
    bm.wait_recv()
    later["cp"].wait_recv()
    total = part[y, top, :] + landed[1] + landed[2]
    out[y, top, :] = jnp.dot(total, inv[...], preferred_element_type=F32, precision=HIGHEST).astype(BF16)
    up0 = go(out.at[y, top], out.at[y, top], yp)
    um0 = go(out.at[y, top], out.at[y, top], ym)
    bp.wait_recv()
    later["cm"].wait_recv()
    total = part[y, low, :] + landed[0] + landed[3]
    out[y, low, :] = jnp.dot(total, inv[...], preferred_element_type=F32, precision=HIGHEST).astype(BF16)
    um1 = go(out.at[y, low], out.at[y, low], ym)
    up1 = go(out.at[y, low], out.at[y, low], yp)

    def over_x(k, part, came, held, slots, rows):
        k.wait_recv()
        held[...] = (part[c] + came[...]).reshape(NX, rows, 128)
        return [go(held.at[lax.rem(x + d, NX)], slots.at[d - 1], xs[d - 1]) for d in range(1, NX)]

    def over_z(copies, held, slots, split, zslots, rows):
        total = held[x]
        for d, copy in enumerate(copies):
            copy.wait_recv()
            total = total + slots[d]
        for i in range(NZ):
            split[i] = total[i * rows : (i + 1) * rows, :]
        return [go(split.at[lax.rem(z + d, NZ)], zslots.at[d - 1], zs[d - 1]) for d in range(1, NZ)]

    def sum_z(copies, split, zslots):
        total = split[z]
        for d, copy in enumerate(copies):
            copy.wait_recv()
            total = total + zslots[d]
        return total

    def back_z(total, place):
        place[c, x, z] = total
        return [go(place.at[c, x, z], place.at[c, x, z], zs[d - 1]) for d in range(1, NZ)]

    def back_x(copies, place):
        for copy in copies:
            copy.wait_recv()
        return [go(place.at[c, x], place.at[c, x], xs[d - 1]) for d in range(1, NX)]

    def back_c(copies, place):
        for copy in copies:
            copy.wait_recv()
        return go(place.at[c], place.at[c], sib)

    whole = gram(out[y], out[y])
    pg[0] = whole[:, :128]
    pg[1] = whole[:, 128:]
    kg = go(pg.at[other], cg, sib)
    ag = over_x(kg, pg, cg, sg, xg, 64)
    up0.wait_recv()
    vp = go(out.at[before, top], out.at[before, top], yp)
    bg = over_z(ag, sg, xg, tg, zg, 4)
    um0.wait_recv()
    um1.wait_recv()
    vm = go(out.at[after, low], out.at[after, low], ym)
    yg[0] = sum_z(bg, tg, zg)
    hy = [go(yg.at[0], yg.at[1], yp), go(yg.at[0], yg.at[2], ym), go(yg.at[0], yg.at[3], y2)]
    up1.wait_recv()
    vp.wait_recv()
    vm.wait_recv()
    rows = out[...].reshape(SLAB, R)
    whole = gram(profile[...], rows)
    pf[0] = whole[:, :128]
    pf[1] = whole[:, 128:]
    kf = go(pf.at[other], cf, sib)
    for copy in hy:
        copy.wait_recv()
    hg = back_z((yg[0] + yg[3]) + (yg[1] + yg[2]), outg)
    af = over_x(kf, pf, cf, sf, xf, 128)
    ig = back_x(hg, outg)
    bf = over_z(af, sf, xf, tf, zf, 8)
    back_c(ig, outg).wait_recv()
    for half in range(2):
        for i in range(NX):
            for j in range(NZ):
                at = i * 64 + j * 4
                inv[at : at + 4, half * 128 : (half + 1) * 128] = outg[half, i, j]
    inv[...] += RIDGE * eye()

    def third():
        later["z"] = back_z(sum_z(bf, tf, zf), outf)

    def fourth():
        later["x"] = back_x(later["z"], outf)

    def fifth():
        later["c"] = back_c(later["x"], outf)

    invert(inv, ((1, third), (4, fourth), (6, fifth)))
    later["c"].wait_recv()
    total = jnp.dot(outf[0].reshape(512, 128), inv[0:128, :], preferred_element_type=F32, precision=HIGHEST)
    total = total + jnp.dot(outf[1].reshape(512, 128), inv[128:, :], preferred_element_type=F32, precision=HIGHEST)
    new[...] = total.astype(BF16)
    go.finish()


VM = pl.BlockSpec(memory_space=pltpu.VMEM)
SM = pl.BlockSpec(memory_space=pltpu.SMEM)


def remote_params(number):
    return pltpu.CompilerParams(collective_id=number, has_side_effects=True, vmem_limit_bytes=VMEM_LIMIT)


PLAIN = pltpu.CompilerParams(vmem_limit_bytes=VMEM_LIMIT)


def shape(dims, dtype):
    return jax.ShapeDtypeStruct(dims, dtype)


def sems(n):
    return [pltpu.SemaphoreType.DMA((n,)), pltpu.SemaphoreType.DMA((n,))]


def local(
    tile_users,
    tile_owners,
    tile_blocks,
    tile_contexts,
    row_users,
    row_items,
    row_contexts,
    tile_values,
    tile_count,
    item_factors,
    context_factors,
    profile,
    feature_factors,
):
    tab, fall = pl.pallas_call(
        gather_kernel,
        out_shape=(shape((2, NZ, NX, 64, R), BF16), shape((2, 3, 256, R), BF16)),
        in_specs=[VM, VM],
        out_specs=(VM, VM),
        scratch_shapes=sems(96),
        compiler_params=remote_params(0),
        name="gather_items",
    )(item_factors, feature_factors)
    tab = tab.reshape(8192, R)
    fall = fall.reshape(1536, R)
    part = pl.pallas_call(
        tile_kernel,
        out_shape=shape((SLAB, R), F32),
        in_specs=[SM] * 5 + [VM] * 8,
        out_specs=VM,
        scratch_shapes=[pltpu.VMEM((TILES * TR, R), BF16), pltpu.VMEM((TILES * TR, R), BF16)],
        compiler_params=PLAIN,
        name="tiles",
    )(
        tile_owners.reshape(TILES),
        tile_blocks.reshape(TILES),
        tile_contexts.reshape(TILES),
        tile_users.reshape(TILES),
        tile_count.reshape(1),
        tab,
        context_factors,
        row_contexts.reshape(TILES, TR),
        row_items.reshape(TILES, TR),
        row_users.reshape(TILES, TR),
        tile_values.reshape(TILES, TR),
        profile,
        feature_factors,
    )
    uf, feature_new = pl.pallas_call(
        factor_kernel,
        out_shape=(shape((NY, 512, R), BF16), shape((512, R), BF16)),
        in_specs=[VM] * 6,
        out_specs=(VM, VM),
        scratch_shapes=[
            pltpu.VMEM((R, R), F32),
            pltpu.VMEM((4, 256, R), F32),
            pltpu.VMEM((4, 256, R), F32),
            pltpu.VMEM((2, NX, NZ, 4, 128), F32),
            pltpu.VMEM((2, NX, NZ, 8, 128), F32),
            pltpu.VMEM((2, 256, 128), F32),
            pltpu.VMEM((2, 512, 128), F32),
            pltpu.VMEM((256, 128), F32),
            pltpu.VMEM((512, 128), F32),
            pltpu.VMEM((NX, 64, 128), F32),
            pltpu.VMEM((NX, 128, 128), F32),
            pltpu.VMEM((3, 64, 128), F32),
            pltpu.VMEM((3, 128, 128), F32),
            pltpu.VMEM((NZ, 4, 128), F32),
            pltpu.VMEM((NZ, 8, 128), F32),
            pltpu.VMEM((NZ - 1, 4, 128), F32),
            pltpu.VMEM((NZ - 1, 8, 128), F32),
            pltpu.VMEM((4, 4, 128), F32),
        ]
        + sems(92),
        compiler_params=remote_params(1),
        name="factors",
    )(part.reshape(NY, 512, R), tab, context_factors, feature_factors, fall, profile)
    return (uf.reshape(SLAB, R), feature_new)


def solution(mesh):
    in_specs = (
        P("users", "items", None),
        P("users", "items", None, None),
        P("users", "items", None),
        P("users", "items", None),
        P("users", "items", None, None),
        P("users", "items", None, None),
        P("users", "items", None, None),
        P("users", "items", None, None),
        P("users", "items"),
        P("users", None),
        P(),
        P("users", "items"),
        P("items", None),
    )
    out_specs = (P("users", None), P("items", None))
    return jax.shard_map(local, mesh=mesh, in_specs=in_specs, out_specs=out_specs, check_vma=False)
```

```python
import functools

import jax
import jax.numpy as jnp
from jax import lax
from jax.experimental import pallas as pl
from jax.experimental.pallas import tpu as pltpu
from jax.sharding import PartitionSpec as P

NZ, NX, NC, NY = 16, 4, 2, 4
R = 256
CB, IB, UB, TR = 128, 16, 16, 128
TILES = 128
SLAB = 2048
RIDGE = 1.0
MESH = pl.DeviceIdType.MESH
F32 = jnp.float32
BF16 = jnp.bfloat16
HIGHEST = lax.Precision.HIGHEST
VMEM_LIMIT = 56 * 1024 * 1024


def position():
    u = lax.axis_index("users")
    y = lax.axis_index("items")
    return lax.div(u, 8), lax.rem(lax.div(u, 2), 4), lax.rem(u, 2), y


def neighbour(dz=0, dx=0, dc=0, dy=0):
    z, x, c, y = position()
    zz = lax.rem(z + dz + NZ, NZ)
    xx = lax.rem(x + dx + NX, NX)
    cc = lax.rem(c + dc, NC)
    return (zz * 8 + xx * 2 + cc, lax.rem(y + dy + NY, NY))


def greet(devices):
    barrier = pltpu.get_barrier_semaphore()
    for device in devices:
        pl.semaphore_signal(barrier, inc=1, device_id=device, device_id_type=MESH)
    return lambda: pl.semaphore_wait(barrier, len(devices))


class Sender:
    def __init__(self, send_sem, recv_sem):
        self.send_sem, self.recv_sem, self.sent = send_sem, recv_sem, []

    def __call__(self, src, dst, device):
        i = len(self.sent)
        copy = pltpu.make_async_remote_copy(
            src_ref=src,
            dst_ref=dst,
            send_sem=self.send_sem.at[i],
            recv_sem=self.recv_sem.at[i],
            device_id=device,
            device_id_type=MESH,
        )
        copy.start()
        self.sent.append(copy)
        return copy

    def finish(self):
        for copy in self.sent:
            copy.wait_send()


def item_place(owner, block, z, x, c):
    rel_z = jnp.bitwise_and(lax.shift_right_logical(owner, 3) - z + NZ, NZ - 1)
    rel_x = jnp.bitwise_and(lax.shift_right_logical(owner, 1) - x + NX, NX - 1)
    rel_c = jnp.bitwise_and(owner + c, 1)
    return ((rel_c * NZ + rel_z) * NX + rel_x) * 4 + block


GROUP = 16


def sweep(block, group):
    panel, size = block.shape
    lane = lax.broadcasted_iota(jnp.int32, (panel, size), 1)
    lane1 = lax.broadcasted_iota(jnp.int32, (1, size), 1)
    sub = lax.broadcasted_iota(jnp.int32, (panel, size), 0)
    sub1 = lax.broadcasted_iota(jnp.int32, (panel, 128), 0)

    def wide(v):
        return jnp.concatenate([v] * (size // 128), axis=1)

    for base in range(0, panel, group):
        columns = [jnp.broadcast_to(block[:, base + j : base + j + 1], (panel, 128)) for j in range(group)]
        for k in range(group):
            at = base + k
            pivot = 1.0 / columns[k][at : at + 1, :]
            row = jnp.where(lane1 == at, wide(pivot), block[at : at + 1, :] * wide(pivot))
            block = jnp.where(sub == at, row, jnp.where(lane == at, 0.0, block) - wide(columns[k]) * row)
            for j in range(k + 1, group):
                factor = columns[j][at : at + 1, :] * pivot
                columns[j] = jnp.where(sub1 == at, factor, columns[j] - columns[k] * factor)
    return block


def invert(ref, between=(), size=R, panel=32, group=16):
    hooks = dict(between)
    lane = lax.broadcasted_iota(jnp.int32, (size - panel, size), 1)

    def step(p, carry):
        block = sweep(ref[0:panel, :], group)
        rest = ref[panel:, :]
        update = jnp.dot(rest[:, 0:panel], block, preferred_element_type=F32, precision=HIGHEST)
        ref[0 : size - panel, :] = pltpu.roll(jnp.where(lane < panel, 0.0, rest) - update, size - panel, 1)
        ref[size - panel :, :] = pltpu.roll(block, size - panel, 1)
        return carry

    done = 0
    for p in sorted(set(hooks) | {size // panel - 1}):
        lax.fori_loop(done, p + 1, step, 0)
        done = p + 1
        if p in hooks:
            hooks[p]()


def eye(size=R):
    return (
        lax.broadcasted_iota(jnp.int32, (size, size), 0) == lax.broadcasted_iota(jnp.int32, (size, size), 1)
    ).astype(F32)


def gram(a, b):
    return lax.dot_general(a, b, (((0,), (0,)), ((), ())), preferred_element_type=F32)


def whole_kernel(
    owners, blocks, tile_contexts, count, item_ref, contexts, row_contexts, row_items, row_users, tile_users, values, profile, features,
    out, new,
    tab, fall, high, low, across_profile, part, sums,
    inv, passing, landed, outg, outf, pg, pf, cg, cf, sg, sf, xg, xf, tg, tf, zg, zf, yg, send_sem, recv_sem,
):
    z, x, c, y = position()
    yp, ym, y2 = neighbour(dy=1), neighbour(dy=-1), neighbour(dy=2)
    zp, zm, sib = neighbour(dz=1), neighbour(dz=-1), neighbour(dc=1)
    xs = [neighbour(dx=d) for d in range(1, NX)]
    zs = [neighbour(dz=d) for d in range(1, NZ)]
    other = lax.rem(c + 1, 2)
    barrier = greet([yp, ym, y2, sib] + xs + zs)
    go = Sender(send_sem, recv_sem)
    later = {}
    tab[0:4] = item_ref[...]

    def own_part(i, carry):
        rows = pl.ds(pl.multiple_of(i * 256, 256), 256)
        product = jnp.dot(profile[rows, :], features[...], preferred_element_type=F32)
        part[0, rows, :] = product[:, :128]
        part[1, rows, :] = product[:, 128:]
        return carry

    lane128 = lax.broadcasted_iota(jnp.int32, (TR, CB), 1)
    lane16 = lax.broadcasted_iota(jnp.int32, (TR, IB), 1)
    sub16 = lax.broadcasted_iota(jnp.int32, (UB, TR), 0)

    def group_rows(g):
        return pl.ds(pl.multiple_of(g * GROUP, GROUP), GROUP)

    def tile_rows(at):
        return pl.ds(pl.multiple_of(at * TR, TR), TR)

    def context_rows(g, carry):
        key = jnp.transpose(row_contexts[group_rows(g), :])
        for t in range(GROUP):
            onehot = (jnp.broadcast_to(key[:, t : t + 1], (TR, CB)) == lane128).astype(F32).astype(BF16)
            at = g * GROUP + t
            block = contexts[tile_contexts[at]]
            high[tile_rows(at), :] = jnp.dot(onehot, block, preferred_element_type=F32).astype(BF16)
        return carry

    def turn(i, carry):
        rows = pl.ds(pl.multiple_of(i * 256, 256), 256)
        across_profile[:, rows] = jnp.transpose(profile[rows, :])
        return carry

    def idle(fn, first, last):
        lax.fori_loop(first, last, fn, 0)

    idle(own_part, 0, 8)
    idle(context_rows, 0, 1)
    barrier()

    def place(core, d, e, n=1):
        return tab.at[pl.ds(((core * NZ + d) * NX + e) * 4, 4 * n)]

    def up(s, e):
        return go(place(0, (-s) % 16, e), place(0, (-s - 1) % 16, e), zp)

    def down(s, e):
        return go(place(0, s, e), place(0, s + 1, e), zm)

    def share(d):
        return go(place(0, d, 0, 4), place(1, d, 0, 4), sib)

    own = place(0, 0, 0)
    arrivals = {3: go(own, place(0, 0, 3), xs[0]), 1: go(own, place(0, 0, 1), xs[2]), 2: go(own, place(0, 0, 2), xs[1])}
    ups, downs = {0: up(0, 0)}, {0: down(0, 0)}
    rows = pl.ds(pl.multiple_of(c * 256, 256), 256)
    feats = [
        go(features.at[rows], fall.at[pl.ds(512, 256)], yp),
        go(features.at[rows], fall.at[pl.ds(0, 256)], ym),
        go(features.at[rows], fall.at[pl.ds(256, 256)], y2),
    ]
    order = (0, 3, 1, 2)
    for e in order[1:]:
        arrivals[e].wait_recv()
        ups[e], downs[e] = up(0, e), down(0, e)
    shared = [share(0)]
    for s in range(8):
        if s < 7:
            idle(context_rows, s + 1, s + 2)
        idle(turn, s, s + 1)
        for e in order:
            if e in ups:
                ups.pop(e).wait_recv()
                if s < 6 or (s == 6 and e in (0, 3)):
                    ups[e] = up(s + 1, e)
            if e in downs:
                downs.pop(e).wait_recv()
                if s < 6 or (s == 6 and e in (1, 2)):
                    downs[e] = down(s + 1, e)
        shared.append(share(s + 1))
        if s < 7:
            shared.append(share(15 - s))
        if s == 5:
            for copy in feats:
                copy.wait_recv()
            shared.append(go(fall.at[pl.ds(0, 768)], fall.at[pl.ds(768, 768)], sib))
    for copy in shared:
        copy.wait_recv()

    def products(g, carry):
        key = jnp.transpose(row_items[group_rows(g), :])
        for t in range(GROUP):
            onehot = (jnp.broadcast_to(key[:, t : t + 1], (TR, IB)) == lane16).astype(F32).astype(BF16)
            at = g * GROUP + t
            block = tab[item_place(owners[at], blocks[at], z, x, c)]
            product = jnp.dot(onehot, block, preferred_element_type=F32) * high[tile_rows(at), :].astype(F32)
            top = product.astype(BF16)
            high[tile_rows(at), :] = top
            low[tile_rows(at), :] = (product - top.astype(F32)).astype(BF16)
        return carry

    lax.fori_loop(0, TILES // GROUP, products, 0)
    live = jnp.broadcast_to(count[...], (GROUP, TR))
    order16 = lax.broadcasted_iota(jnp.int32, (GROUP, TR), 0)
    to_block = (lax.broadcasted_iota(jnp.int32, (128, TILES), 0) == jnp.broadcast_to(tile_users[...], (128, TILES))).astype(F32)
    to_block = jnp.concatenate([to_block.astype(BF16)] * 3, axis=1)
    after, before, across = lax.rem(y + 1, NY), lax.rem(y + 3, NY), lax.rem(y + 2, NY)

    def top(q):
        return pl.ds(pl.multiple_of(q * 512, 512), 256)

    def bottom(q):
        return pl.ds(pl.multiple_of(q * 512 + 256, 256), 256)

    def add_tiles(h):
        columns = slice(h * 128, h * 128 + 128)

        def tile_sums(g, carry):
            user = row_users[group_rows(g), :]
            value = jnp.where(order16 + g * GROUP < live, values[group_rows(g), :].astype(F32), 0.0)
            for t in range(GROUP):
                at = g * GROUP + t
                weight = jnp.where(user[t : t + 1, :] == sub16, value[t : t + 1, :], 0.0).astype(BF16)
                sums[group_rows(at), :] = jnp.dot(
                    weight, high[tile_rows(at), columns], preferred_element_type=F32
                ) + jnp.dot(weight, low[tile_rows(at), columns], preferred_element_type=F32)
            return carry

        lax.fori_loop(0, TILES // GROUP, tile_sums, 0)
        for u in range(UB):
            rows = pl.ds(u, 128, stride=UB)
            value = sums[rows, :]
            first = value.astype(BF16)
            value = value - first.astype(F32)
            second = value.astype(BF16)
            third = (value - second.astype(F32)).astype(BF16)
            total = jnp.dot(to_block, jnp.concatenate([first, second, third], axis=0), preferred_element_type=F32)
            sums[rows, :] = total
        part[h] += sums[...]
        ap = go(part.at[h, top(across)], passing.at[h, 0], yp)
        am = go(part.at[h, bottom(across)], passing.at[h, 1], ym)
        bp = go(part.at[h, bottom(after)], landed.at[h, 0], yp)
        bm = go(part.at[h, top(before)], landed.at[h, 1], ym)

        def relay():
            ap.wait_recv()
            passing[h, 2] = passing[h, 0] + part[h, top(after), :]
            cp = go(passing.at[h, 2], landed.at[h, 2], yp)
            am.wait_recv()
            passing[h, 3] = passing[h, 1] + part[h, bottom(before), :]
            cm = go(passing.at[h, 3], landed.at[h, 3], ym)
            later[h] = (bm, cp, bp, cm)

        return relay

    relays = [add_tiles(0), add_tiles(1)]
    def item_gram(i, acc):
        rows = tab[pl.ds(pl.multiple_of(i * 64, 64), 64)].reshape(1024, R)
        return acc + gram(rows, rows)

    items = lax.fori_loop(0, 8, item_gram, jnp.zeros((R, R), F32))
    table = contexts[...].reshape(1024, R)
    relays[0]()
    normal = items * gram(table, table) + gram(features[...], features[...])
    inv[...] = normal + gram(fall[...], fall[...]) + RIDGE * eye()
    invert(inv, ((1, relays[1]),))

    def solve(rows, copies, one, two):
        total = jnp.zeros((256, R), F32)
        for h in range(2):
            for i in copies:
                later[h][i].wait_recv()
            right = part[h, rows, :] + landed[h, one] + landed[h, two]
            total = total + jnp.dot(
                right, inv[h * 128 : h * 128 + 128, :], preferred_element_type=F32, precision=HIGHEST
            )
        out[rows, :] = total.astype(BF16)

    solve(top(y), (0, 1), 1, 2)
    up0 = go(out.at[top(y)], out.at[top(y)], yp)
    um0 = go(out.at[top(y)], out.at[top(y)], ym)
    solve(bottom(y), (2, 3), 0, 3)
    um1 = go(out.at[bottom(y)], out.at[bottom(y)], ym)
    up1 = go(out.at[bottom(y)], out.at[bottom(y)], yp)

    def over_x(k, part, came, held, slots, rows):
        k.wait_recv()
        held[...] = (part[c] + came[...]).reshape(NX, rows, 128)
        return [go(held.at[lax.rem(x + d, NX)], slots.at[d - 1], xs[d - 1]) for d in range(1, NX)]

    def over_z(copies, held, slots, split, zslots, rows):
        total = held[x]
        for d, copy in enumerate(copies):
            copy.wait_recv()
            total = total + slots[d]
        for i in range(NZ):
            split[i] = total[i * rows : (i + 1) * rows, :]
        return [go(split.at[lax.rem(z + d, NZ)], zslots.at[d - 1], zs[d - 1]) for d in range(1, NZ)]

    def sum_z(copies, split, zslots):
        total = split[z]
        for d, copy in enumerate(copies):
            copy.wait_recv()
            total = total + zslots[d]
        return total

    def back_z(total, place):
        place[c, x, z] = total
        return [go(place.at[c, x, z], place.at[c, x, z], zs[d - 1]) for d in range(1, NZ)]

    def back_x(copies, place):
        for copy in copies:
            copy.wait_recv()
        return [go(place.at[c, x], place.at[c, x], xs[d - 1]) for d in range(1, NX)]

    def back_c(copies, place):
        for copy in copies:
            copy.wait_recv()
        return go(place.at[c], place.at[c], sib)

    mine = out[pl.ds(pl.multiple_of(y * 512, 512), 512), :]
    whole = gram(mine, mine)
    pg[0] = whole[:, :128]
    pg[1] = whole[:, 128:]
    kg = go(pg.at[other], cg, sib)
    ag = over_x(kg, pg, cg, sg, xg, 64)
    up0.wait_recv()
    vp = go(out.at[top(before)], out.at[top(before)], yp)
    bg = over_z(ag, sg, xg, tg, zg, 4)
    um0.wait_recv()
    um1.wait_recv()
    vm = go(out.at[bottom(after)], out.at[bottom(after)], ym)
    yg[0] = sum_z(bg, tg, zg)
    hy = [go(yg.at[0], yg.at[1], yp), go(yg.at[0], yg.at[2], ym), go(yg.at[0], yg.at[3], y2)]
    up1.wait_recv()
    vp.wait_recv()
    vm.wait_recv()
    whole = jnp.dot(across_profile[...], out[...], preferred_element_type=F32)
    pf[0] = whole[:, :128]
    pf[1] = whole[:, 128:]
    kf = go(pf.at[other], cf, sib)
    for copy in hy:
        copy.wait_recv()
    hg = back_z((yg[0] + yg[3]) + (yg[1] + yg[2]), outg)
    af = over_x(kf, pf, cf, sf, xf, 128)
    ig = back_x(hg, outg)
    bf = over_z(af, sf, xf, tf, zf, 8)
    back_c(ig, outg).wait_recv()
    for half in range(2):
        for i in range(NX):
            for j in range(NZ):
                at = i * 64 + j * 4
                inv[at : at + 4, half * 128 : (half + 1) * 128] = outg[half, i, j]
    inv[...] += RIDGE * eye()

    def third():
        later["z"] = back_z(sum_z(bf, tf, zf), outf)

    def fourth():
        later["x"] = back_x(later["z"], outf)

    def fifth():
        later["c"] = back_c(later["x"], outf)

    invert(inv, ((1, third), (4, fourth), (6, fifth)))
    later["c"].wait_recv()
    total = jnp.dot(outf[0].reshape(512, 128), inv[0:128, :], preferred_element_type=F32, precision=HIGHEST)
    total = total + jnp.dot(outf[1].reshape(512, 128), inv[128:, :], preferred_element_type=F32, precision=HIGHEST)
    new[...] = total.astype(BF16)
    go.finish()


VM = pl.BlockSpec(memory_space=pltpu.VMEM)
SM = pl.BlockSpec(memory_space=pltpu.SMEM)


def remote_params(number):
    return pltpu.CompilerParams(collective_id=number, has_side_effects=True, vmem_limit_bytes=VMEM_LIMIT)


PLAIN = pltpu.CompilerParams(vmem_limit_bytes=VMEM_LIMIT)


def shape(dims, dtype):
    return jax.ShapeDtypeStruct(dims, dtype)


def sems(n):
    return [pltpu.SemaphoreType.DMA((n,)), pltpu.SemaphoreType.DMA((n,))]


def local(
    tile_users,
    tile_owners,
    tile_blocks,
    tile_contexts,
    row_users,
    row_items,
    row_contexts,
    tile_values,
    tile_count,
    item_factors,
    context_factors,
    profile,
    feature_factors,
):
    return tuple(
        pl.pallas_call(
            whole_kernel,
            out_shape=(shape((SLAB, R), BF16), shape((512, R), BF16)),
            in_specs=[SM] * 3 + [VM] * 10,
            out_specs=(VM, VM),
            scratch_shapes=[
                pltpu.VMEM((512, IB, R), BF16),
                pltpu.VMEM((1536, R), BF16),
                pltpu.VMEM((TILES * TR, R), BF16),
                pltpu.VMEM((TILES * TR, R), BF16),
                pltpu.VMEM((512, SLAB), BF16),
                pltpu.VMEM((2, SLAB, 128), F32),
                pltpu.VMEM((SLAB, 128), F32),
                pltpu.VMEM((R, R), F32),
                pltpu.VMEM((2, 4, 256, 128), F32),
                pltpu.VMEM((2, 4, 256, 128), F32),
                pltpu.VMEM((2, NX, NZ, 4, 128), F32),
                pltpu.VMEM((2, NX, NZ, 8, 128), F32),
                pltpu.VMEM((2, 256, 128), F32),
                pltpu.VMEM((2, 512, 128), F32),
                pltpu.VMEM((256, 128), F32),
                pltpu.VMEM((512, 128), F32),
                pltpu.VMEM((NX, 64, 128), F32),
                pltpu.VMEM((NX, 128, 128), F32),
                pltpu.VMEM((3, 64, 128), F32),
                pltpu.VMEM((3, 128, 128), F32),
                pltpu.VMEM((NZ, 4, 128), F32),
                pltpu.VMEM((NZ, 8, 128), F32),
                pltpu.VMEM((NZ - 1, 4, 128), F32),
                pltpu.VMEM((NZ - 1, 8, 128), F32),
                pltpu.VMEM((4, 4, 128), F32),
            ]
    + sems(200),
            compiler_params=remote_params(0),
            name="whole",
        )(
            tile_owners.reshape(TILES),
            tile_blocks.reshape(TILES),
            tile_contexts.reshape(TILES),
            tile_count,
            item_factors.reshape(4, IB, R),
            context_factors.reshape(8, CB, R),
            row_contexts.reshape(TILES, TR),
            row_items.reshape(TILES, TR),
            row_users.reshape(TILES, TR),
            tile_users.reshape(1, TILES),
            tile_values.reshape(TILES, TR),
            profile,
            feature_factors,
        )
    )


def solution(mesh):
    in_specs = (
        P("users", "items", None),
        P("users", "items", None, None),
        P("users", "items", None),
        P("users", "items", None),
        P("users", "items", None, None),
        P("users", "items", None, None),
        P("users", "items", None, None),
        P("users", "items", None, None),
        P("users", "items"),
        P("users", None),
        P(),
        P("users", "items"),
        P("items", None),
    )
    out_specs = (P("users", None), P("items", None))
    return jax.shard_map(local, mesh=mesh, in_specs=in_specs, out_specs=out_specs, check_vma=False)
```

```python
import functools

import jax
import jax.numpy as jnp
from jax import lax
from jax.experimental import pallas as pl
from jax.experimental.pallas import tpu as pltpu
from jax.sharding import PartitionSpec as P

NZ, NX, NC, NY = 16, 4, 2, 4
R = 256
CB, IB, UB, TR = 128, 16, 16, 128
TILES = 128
SLAB = 2048
RIDGE = 1.0
MESH = pl.DeviceIdType.MESH
F32 = jnp.float32
BF16 = jnp.bfloat16
HIGHEST = lax.Precision.HIGHEST
VMEM_LIMIT = 56 * 1024 * 1024


def position():
    u = lax.axis_index("users")
    y = lax.axis_index("items")
    return lax.div(u, 8), lax.rem(lax.div(u, 2), 4), lax.rem(u, 2), y


def neighbour(dz=0, dx=0, dc=0, dy=0):
    z, x, c, y = position()
    zz = lax.rem(z + dz + NZ, NZ)
    xx = lax.rem(x + dx + NX, NX)
    cc = lax.rem(c + dc, NC)
    return (zz * 8 + xx * 2 + cc, lax.rem(y + dy + NY, NY))


def greet(devices):
    barrier = pltpu.get_barrier_semaphore()
    for device in devices:
        pl.semaphore_signal(barrier, inc=1, device_id=device, device_id_type=MESH)
    return lambda: pl.semaphore_wait(barrier, len(devices))


class Sender:
    def __init__(self, send_sem, recv_sem):
        self.send_sem, self.recv_sem, self.sent = send_sem, recv_sem, []

    def __call__(self, src, dst, device):
        i = len(self.sent)
        copy = pltpu.make_async_remote_copy(
            src_ref=src,
            dst_ref=dst,
            send_sem=self.send_sem.at[i],
            recv_sem=self.recv_sem.at[i],
            device_id=device,
            device_id_type=MESH,
        )
        copy.start()
        self.sent.append(copy)
        return copy

    def finish(self):
        for copy in self.sent:
            copy.wait_send()


def item_place(owner, block, z, x, c):
    rel_z = jnp.bitwise_and(lax.shift_right_logical(owner, 3) - z + NZ, NZ - 1)
    rel_x = jnp.bitwise_and(lax.shift_right_logical(owner, 1) - x + NX, NX - 1)
    rel_c = jnp.bitwise_and(owner + c, 1)
    return ((rel_c * NZ + rel_z) * NX + rel_x) * 4 + block


GROUP = 16


def sweep(block, group):
    panel, size = block.shape
    lane = lax.broadcasted_iota(jnp.int32, (panel, size), 1)
    lane1 = lax.broadcasted_iota(jnp.int32, (1, size), 1)
    sub = lax.broadcasted_iota(jnp.int32, (panel, size), 0)
    sub1 = lax.broadcasted_iota(jnp.int32, (panel, 128), 0)

    def wide(v):
        return jnp.concatenate([v] * (size // 128), axis=1)

    for base in range(0, panel, group):
        columns = [jnp.broadcast_to(block[:, base + j : base + j + 1], (panel, 128)) for j in range(group)]
        for k in range(group):
            at = base + k
            pivot = 1.0 / columns[k][at : at + 1, :]
            row = jnp.where(lane1 == at, wide(pivot), block[at : at + 1, :] * wide(pivot))
            block = jnp.where(sub == at, row, jnp.where(lane == at, 0.0, block) - wide(columns[k]) * row)
            for j in range(k + 1, group):
                factor = columns[j][at : at + 1, :] * pivot
                columns[j] = jnp.where(sub1 == at, factor, columns[j] - columns[k] * factor)
    return block


def invert(ref, between=(), size=R, panel=32, group=16):
    hooks = dict(between)
    lane = lax.broadcasted_iota(jnp.int32, (size - panel, size), 1)

    def step(p, carry):
        block = sweep(ref[0:panel, :], group)
        rest = ref[panel:, :]
        update = jnp.dot(rest[:, 0:panel], block, preferred_element_type=F32, precision=HIGHEST)
        ref[0 : size - panel, :] = pltpu.roll(jnp.where(lane < panel, 0.0, rest) - update, size - panel, 1)
        ref[size - panel :, :] = pltpu.roll(block, size - panel, 1)
        return carry

    done = 0
    for p in sorted(set(hooks) | {size // panel - 1}):
        lax.fori_loop(done, p + 1, step, 0)
        done = p + 1
        if p in hooks:
            hooks[p]()


def eye(size=R):
    return (
        lax.broadcasted_iota(jnp.int32, (size, size), 0) == lax.broadcasted_iota(jnp.int32, (size, size), 1)
    ).astype(F32)


def gram(a, b):
    return lax.dot_general(a, b, (((0,), (0,)), ((), ())), preferred_element_type=F32)


def whole_kernel(
    owners, blocks, tile_contexts, count, item_ref, contexts, row_contexts, row_items, row_users, tile_users, values, profile, features,
    out, new,
    tab, fall, high, low, across_profile, part, sums,
    inv, passing, landed, outg, outf, pg, pf, cg, cf, sg, sf, xg, xf, tg, tf, zg, zf, yg, send_sem, recv_sem,
):
    z, x, c, y = position()
    yp, ym, y2 = neighbour(dy=1), neighbour(dy=-1), neighbour(dy=2)
    zp, zm, sib = neighbour(dz=1), neighbour(dz=-1), neighbour(dc=1)
    xs = [neighbour(dx=d) for d in range(1, NX)]
    zs = [neighbour(dz=d) for d in range(1, NZ)]
    other = lax.rem(c + 1, 2)
    barrier = greet([yp, ym, y2, sib, zp, zm] + xs)
    go = Sender(send_sem, recv_sem)
    later = {}
    tab[0:4] = item_ref[...]

    def own_part(i, carry):
        rows = pl.ds(pl.multiple_of(i * 256, 256), 256)
        product = jnp.dot(profile[rows, :], features[...], preferred_element_type=F32)
        part[0, rows, :] = product[:, :128]
        part[1, rows, :] = product[:, 128:]
        return carry

    lane128 = lax.broadcasted_iota(jnp.int32, (TR, CB), 1)
    lane16 = lax.broadcasted_iota(jnp.int32, (TR, IB), 1)
    sub16 = lax.broadcasted_iota(jnp.int32, (UB, TR), 0)

    def group_rows(g):
        return pl.ds(pl.multiple_of(g * GROUP, GROUP), GROUP)

    def tile_rows(at):
        return pl.ds(pl.multiple_of(at * TR, TR), TR)

    def context_rows(g, carry):
        key = jnp.transpose(row_contexts[group_rows(g), :])
        for t in range(GROUP):
            onehot = (jnp.broadcast_to(key[:, t : t + 1], (TR, CB)) == lane128).astype(F32).astype(BF16)
            at = g * GROUP + t
            block = contexts[tile_contexts[at]]
            high[tile_rows(at), :] = jnp.dot(onehot, block, preferred_element_type=F32).astype(BF16)
        return carry

    def turn(i, carry):
        rows = pl.ds(pl.multiple_of(i * 256, 256), 256)
        across_profile[:, rows] = jnp.transpose(profile[rows, :])
        return carry

    def idle(fn, first, last):
        lax.fori_loop(first, last, fn, 0)

    idle(own_part, 0, 8)
    idle(context_rows, 0, 1)
    barrier()

    def place(core, d, e, n=1):
        return tab.at[pl.ds(((core * NZ + d) * NX + e) * 4, 4 * n)]

    def up(s, e):
        return go(place(0, (-s) % 16, e), place(0, (-s - 1) % 16, e), zp)

    def down(s, e):
        return go(place(0, s, e), place(0, s + 1, e), zm)

    def share(d):
        return go(place(0, d, 0, 4), place(1, d, 0, 4), sib)

    own = place(0, 0, 0)
    arrivals = {3: go(own, place(0, 0, 3), xs[0]), 1: go(own, place(0, 0, 1), xs[2]), 2: go(own, place(0, 0, 2), xs[1])}
    ups, downs = {0: up(0, 0)}, {0: down(0, 0)}
    rows = pl.ds(pl.multiple_of(c * 256, 256), 256)
    feats = [
        go(features.at[rows], fall.at[pl.ds(512, 256)], yp),
        go(features.at[rows], fall.at[pl.ds(0, 256)], ym),
        go(features.at[rows], fall.at[pl.ds(256, 256)], y2),
    ]
    order = (0, 3, 1, 2)
    for e in order[1:]:
        arrivals[e].wait_recv()
        ups[e], downs[e] = up(0, e), down(0, e)
    shared = [share(0)]
    for s in range(8):
        if s < 7:
            idle(context_rows, s + 1, s + 2)
        idle(turn, s, s + 1)
        for e in order:
            if e in ups:
                ups.pop(e).wait_recv()
                if s < 6 or (s == 6 and e in (0, 3)):
                    ups[e] = up(s + 1, e)
            if e in downs:
                downs.pop(e).wait_recv()
                if s < 6 or (s == 6 and e in (1, 2)):
                    downs[e] = down(s + 1, e)
        shared.append(share(s + 1))
        if s < 7:
            shared.append(share(15 - s))
        if s == 5:
            for copy in feats:
                copy.wait_recv()
            shared.append(go(fall.at[pl.ds(0, 768)], fall.at[pl.ds(768, 768)], sib))
    for copy in shared:
        copy.wait_recv()

    def products(g, carry):
        key = jnp.transpose(row_items[group_rows(g), :])
        for t in range(GROUP):
            onehot = (jnp.broadcast_to(key[:, t : t + 1], (TR, IB)) == lane16).astype(F32).astype(BF16)
            at = g * GROUP + t
            block = tab[item_place(owners[at], blocks[at], z, x, c)]
            product = jnp.dot(onehot, block, preferred_element_type=F32) * high[tile_rows(at), :].astype(F32)
            top = product.astype(BF16)
            high[tile_rows(at), :] = top
            low[tile_rows(at), :] = (product - top.astype(F32)).astype(BF16)
        return carry

    lax.fori_loop(0, TILES // GROUP, products, 0)
    live = jnp.broadcast_to(count[...], (GROUP, TR))
    order16 = lax.broadcasted_iota(jnp.int32, (GROUP, TR), 0)
    to_block = (lax.broadcasted_iota(jnp.int32, (128, TILES), 0) == jnp.broadcast_to(tile_users[...], (128, TILES))).astype(F32)
    to_block = jnp.concatenate([to_block.astype(BF16)] * 3, axis=1)
    after, before, across = lax.rem(y + 1, NY), lax.rem(y + 3, NY), lax.rem(y + 2, NY)

    def top(q):
        return pl.ds(pl.multiple_of(q * 512, 512), 256)

    def bottom(q):
        return pl.ds(pl.multiple_of(q * 512 + 256, 256), 256)

    def add_tiles(h):
        columns = slice(h * 128, h * 128 + 128)

        def tile_sums(g, carry):
            user = row_users[group_rows(g), :]
            value = jnp.where(order16 + g * GROUP < live, values[group_rows(g), :].astype(F32), 0.0)
            for t in range(GROUP):
                at = g * GROUP + t
                weight = jnp.where(user[t : t + 1, :] == sub16, value[t : t + 1, :], 0.0).astype(BF16)
                sums[group_rows(at), :] = jnp.dot(
                    weight, high[tile_rows(at), columns], preferred_element_type=F32
                ) + jnp.dot(weight, low[tile_rows(at), columns], preferred_element_type=F32)
            return carry

        lax.fori_loop(0, TILES // GROUP, tile_sums, 0)
        for u in range(UB):
            rows = pl.ds(u, 128, stride=UB)
            value = sums[rows, :]
            first = value.astype(BF16)
            value = value - first.astype(F32)
            second = value.astype(BF16)
            third = (value - second.astype(F32)).astype(BF16)
            total = jnp.dot(to_block, jnp.concatenate([first, second, third], axis=0), preferred_element_type=F32)
            sums[rows, :] = total
        part[h] += sums[...]
        ap = go(part.at[h, top(across)], passing.at[h, 0], yp)
        am = go(part.at[h, bottom(across)], passing.at[h, 1], ym)
        bp = go(part.at[h, bottom(after)], landed.at[h, 0], yp)
        bm = go(part.at[h, top(before)], landed.at[h, 1], ym)

        def relay():
            ap.wait_recv()
            passing[h, 2] = passing[h, 0] + part[h, top(after), :]
            cp = go(passing.at[h, 2], landed.at[h, 2], yp)
            am.wait_recv()
            passing[h, 3] = passing[h, 1] + part[h, bottom(before), :]
            cm = go(passing.at[h, 3], landed.at[h, 3], ym)
            later[h] = (bm, cp, bp, cm)

        return relay

    relays = [add_tiles(0), add_tiles(1)]
    def item_gram(i, acc):
        rows = tab[pl.ds(pl.multiple_of(i * 64, 64), 64)].reshape(1024, R)
        return acc + gram(rows, rows)

    items = lax.fori_loop(0, 8, item_gram, jnp.zeros((R, R), F32))
    table = contexts[...].reshape(1024, R)
    relays[0]()
    normal = items * gram(table, table) + gram(features[...], features[...])
    inv[...] = normal + gram(fall[...], fall[...]) + RIDGE * eye()
    invert(inv, ((1, relays[1]),))

    def solve(rows, copies, one, two):
        total = jnp.zeros((256, R), F32)
        for h in range(2):
            for i in copies:
                later[h][i].wait_recv()
            right = part[h, rows, :] + landed[h, one] + landed[h, two]
            total = total + jnp.dot(
                right, inv[h * 128 : h * 128 + 128, :], preferred_element_type=F32, precision=HIGHEST
            )
        out[rows, :] = total.astype(BF16)

    solve(top(y), (0, 1), 1, 2)
    up0 = go(out.at[top(y)], out.at[top(y)], yp)
    um0 = go(out.at[top(y)], out.at[top(y)], ym)
    solve(bottom(y), (2, 3), 0, 3)
    um1 = go(out.at[bottom(y)], out.at[bottom(y)], ym)
    up1 = go(out.at[bottom(y)], out.at[bottom(y)], yp)

    def over_x(k, part, came, held, slots, rows):
        k.wait_recv()
        held[...] = (part[c] + came[...]).reshape(NX, rows, 128)
        return [go(held.at[lax.rem(x + d, NX)], slots.at[d - 1], xs[d - 1]) for d in range(1, NX)]

    def over_z(copies, held, slots, split, zslots, rows):
        total = held[x]
        for d, copy in enumerate(copies):
            copy.wait_recv()
            total = total + slots[d]
        for i in range(NZ):
            split[i] = total[i * rows : (i + 1) * rows, :]
        return [go(split.at[lax.rem(z + d, NZ)], zslots.at[d - 1], zs[d - 1]) for d in range(1, NZ)]

    def sum_z(copies, split, zslots):
        total = split[z]
        for d, copy in enumerate(copies):
            copy.wait_recv()
            total = total + zslots[d]
        return total

    def back_z(total, place):
        place[c, x, z] = total
        return [go(place.at[c, x, z], place.at[c, x, z], zs[d - 1]) for d in range(1, NZ)]

    def back_x(copies, place):
        for copy in copies:
            copy.wait_recv()
        return [go(place.at[c, x], place.at[c, x], xs[d - 1]) for d in range(1, NX)]

    def back_c(copies, place):
        for copy in copies:
            copy.wait_recv()
        return go(place.at[c], place.at[c], sib)

    mine = out[pl.ds(pl.multiple_of(y * 512, 512), 512), :]
    whole = gram(mine, mine)
    pg[0] = whole[:, :128]
    pg[1] = whole[:, 128:]
    kg = go(pg.at[other], cg, sib)
    ag = over_x(kg, pg, cg, sg, xg, 64)
    up0.wait_recv()
    vp = go(out.at[top(before)], out.at[top(before)], yp)
    bg = over_z(ag, sg, xg, tg, zg, 4)
    um0.wait_recv()
    um1.wait_recv()
    vm = go(out.at[bottom(after)], out.at[bottom(after)], ym)
    yg[0] = sum_z(bg, tg, zg)
    hy = [go(yg.at[0], yg.at[1], yp), go(yg.at[0], yg.at[2], ym), go(yg.at[0], yg.at[3], y2)]
    up1.wait_recv()
    vp.wait_recv()
    vm.wait_recv()
    whole = jnp.dot(across_profile[...], out[...], preferred_element_type=F32)
    pf[0] = whole[:, :128]
    pf[1] = whole[:, 128:]
    kf = go(pf.at[other], cf, sib)
    for copy in hy:
        copy.wait_recv()
    hg = back_z((yg[0] + yg[3]) + (yg[1] + yg[2]), outg)
    af = over_x(kf, pf, cf, sf, xf, 128)
    bf = over_z(af, sf, xf, tf, zf, 8)
    ig = back_x(hg, outg)
    back_c(ig, outg).wait_recv()
    for half in range(2):
        for i in range(NX):
            for j in range(NZ):
                at = i * 64 + j * 4
                inv[at : at + 4, half * 128 : (half + 1) * 128] = outg[half, i, j]
    inv[...] += RIDGE * eye()

    def third():
        later["z"] = back_z(sum_z(bf, tf, zf), outf)

    def fourth():
        later["x"] = back_x(later["z"], outf)

    def fifth():
        later["c"] = back_c(later["x"], outf)

    invert(inv, ((1, third), (4, fourth), (6, fifth)))
    later["c"].wait_recv()
    total = jnp.dot(outf[0].reshape(512, 128), inv[0:128, :], preferred_element_type=F32, precision=HIGHEST)
    total = total + jnp.dot(outf[1].reshape(512, 128), inv[128:, :], preferred_element_type=F32, precision=HIGHEST)
    new[...] = total.astype(BF16)
    go.finish()


def copy_kernel(uf, new, uf_out, new_out):
    uf_out[...] = uf[...]
    new_out[...] = new[...]


VM = pl.BlockSpec(memory_space=pltpu.VMEM)
SM = pl.BlockSpec(memory_space=pltpu.SMEM)


def remote_params(number):
    return pltpu.CompilerParams(collective_id=number, has_side_effects=True, vmem_limit_bytes=VMEM_LIMIT)


PLAIN = pltpu.CompilerParams(vmem_limit_bytes=VMEM_LIMIT)


def shape(dims, dtype):
    return jax.ShapeDtypeStruct(dims, dtype)


def sems(n):
    return [pltpu.SemaphoreType.DMA((n,)), pltpu.SemaphoreType.DMA((n,))]


def local(
    tile_users,
    tile_owners,
    tile_blocks,
    tile_contexts,
    row_users,
    row_items,
    row_contexts,
    tile_values,
    tile_count,
    item_factors,
    context_factors,
    profile,
    feature_factors,
):
    uf, new = tuple(
        pl.pallas_call(
            whole_kernel,
            out_shape=(shape((SLAB, R), BF16), shape((512, R), BF16)),
            in_specs=[SM] * 3 + [VM] * 10,
            out_specs=(VM, VM),
            scratch_shapes=[
                pltpu.VMEM((512, IB, R), BF16),
                pltpu.VMEM((1536, R), BF16),
                pltpu.VMEM((TILES * TR, R), BF16),
                pltpu.VMEM((TILES * TR, R), BF16),
                pltpu.VMEM((512, SLAB), BF16),
                pltpu.VMEM((2, SLAB, 128), F32),
                pltpu.VMEM((SLAB, 128), F32),
                pltpu.VMEM((R, R), F32),
                pltpu.VMEM((2, 4, 256, 128), F32),
                pltpu.VMEM((2, 4, 256, 128), F32),
                pltpu.VMEM((2, NX, NZ, 4, 128), F32),
                pltpu.VMEM((2, NX, NZ, 8, 128), F32),
                pltpu.VMEM((2, 256, 128), F32),
                pltpu.VMEM((2, 512, 128), F32),
                pltpu.VMEM((256, 128), F32),
                pltpu.VMEM((512, 128), F32),
                pltpu.VMEM((NX, 64, 128), F32),
                pltpu.VMEM((NX, 128, 128), F32),
                pltpu.VMEM((3, 64, 128), F32),
                pltpu.VMEM((3, 128, 128), F32),
                pltpu.VMEM((NZ, 4, 128), F32),
                pltpu.VMEM((NZ, 8, 128), F32),
                pltpu.VMEM((NZ - 1, 4, 128), F32),
                pltpu.VMEM((NZ - 1, 8, 128), F32),
                pltpu.VMEM((4, 4, 128), F32),
            ]
    + sems(200),
            compiler_params=remote_params(0),
            name="whole",
        )(
            tile_owners.reshape(TILES),
            tile_blocks.reshape(TILES),
            tile_contexts.reshape(TILES),
            tile_count,
            item_factors.reshape(4, IB, R),
            context_factors.reshape(8, CB, R),
            row_contexts.reshape(TILES, TR),
            row_items.reshape(TILES, TR),
            row_users.reshape(TILES, TR),
            tile_users.reshape(1, TILES),
            tile_values.reshape(TILES, TR),
            profile,
            feature_factors,
        )
    )
    return tuple(
        pl.pallas_call(
            copy_kernel,
            out_shape=(shape((SLAB, R), BF16), shape((512, R), BF16)),
            in_specs=[VM, VM],
            out_specs=(VM, VM),
            compiler_params=PLAIN,
            name="results",
        )(uf, new)
    )


def solution(mesh):
    in_specs = (
        P("users", "items", None),
        P("users", "items", None, None),
        P("users", "items", None),
        P("users", "items", None),
        P("users", "items", None, None),
        P("users", "items", None, None),
        P("users", "items", None, None),
        P("users", "items", None, None),
        P("users", "items"),
        P("users", None),
        P(),
        P("users", "items"),
        P("items", None),
    )
    out_specs = (P("users", None), P("items", None))
    return jax.shard_map(local, mesh=mesh, in_specs=in_specs, out_specs=out_specs, check_vma=False)
```

```python
import functools

import jax
import jax.numpy as jnp
from jax import lax
from jax.experimental import pallas as pl
from jax.experimental.pallas import tpu as pltpu
from jax.sharding import PartitionSpec as P

NZ, NX, NC, NY = 16, 4, 2, 4
R = 256
CB, IB, UB, TR = 128, 16, 16, 128
TILES = 128
SLAB = 2048
RIDGE = 1.0
MESH = pl.DeviceIdType.MESH
F32 = jnp.float32
BF16 = jnp.bfloat16
HIGHEST = lax.Precision.HIGHEST
VMEM_LIMIT = 56 * 1024 * 1024


def position():
    u = lax.axis_index("users")
    y = lax.axis_index("items")
    return lax.div(u, 8), lax.rem(lax.div(u, 2), 4), lax.rem(u, 2), y


def neighbour(dz=0, dx=0, dc=0, dy=0):
    z, x, c, y = position()
    zz = lax.rem(z + dz + NZ, NZ)
    xx = lax.rem(x + dx + NX, NX)
    cc = lax.rem(c + dc, NC)
    return (zz * 8 + xx * 2 + cc, lax.rem(y + dy + NY, NY))


def greet(devices):
    barrier = pltpu.get_barrier_semaphore()
    for device in devices:
        pl.semaphore_signal(barrier, inc=1, device_id=device, device_id_type=MESH)
    return lambda: pl.semaphore_wait(barrier, len(devices))


def farthest_first(n, start):
    copies = {}
    for d in sorted(range(1, n), key=lambda d: -min(d, n - d)):
        copies[d] = start(d)
    return [copies[d] for d in range(1, n)]


class Sender:
    def __init__(self, send_sem, recv_sem):
        self.send_sem, self.recv_sem, self.sent = send_sem, recv_sem, []

    def __call__(self, src, dst, device):
        i = len(self.sent)
        copy = pltpu.make_async_remote_copy(
            src_ref=src,
            dst_ref=dst,
            send_sem=self.send_sem.at[i],
            recv_sem=self.recv_sem.at[i],
            device_id=device,
            device_id_type=MESH,
        )
        copy.start()
        self.sent.append(copy)
        return copy

    def finish(self):
        for copy in self.sent:
            copy.wait_send()


def item_place(owner, block, z, x, c):
    rel_z = jnp.bitwise_and(lax.shift_right_logical(owner, 3) - z + NZ, NZ - 1)
    rel_x = jnp.bitwise_and(lax.shift_right_logical(owner, 1) - x + NX, NX - 1)
    rel_c = jnp.bitwise_and(owner + c, 1)
    return ((rel_c * NZ + rel_z) * NX + rel_x) * 4 + block


GROUP = 16


def sweep(block, group):
    panel, size = block.shape
    lane = lax.broadcasted_iota(jnp.int32, (panel, size), 1)
    lane1 = lax.broadcasted_iota(jnp.int32, (1, size), 1)
    sub = lax.broadcasted_iota(jnp.int32, (panel, size), 0)
    sub1 = lax.broadcasted_iota(jnp.int32, (panel, 128), 0)

    def wide(v):
        return jnp.concatenate([v] * (size // 128), axis=1)

    for base in range(0, panel, group):
        columns = [jnp.broadcast_to(block[:, base + j : base + j + 1], (panel, 128)) for j in range(group)]
        for k in range(group):
            at = base + k
            pivot = 1.0 / columns[k][at : at + 1, :]
            row = jnp.where(lane1 == at, wide(pivot), block[at : at + 1, :] * wide(pivot))
            block = jnp.where(sub == at, row, jnp.where(lane == at, 0.0, block) - wide(columns[k]) * row)
            for j in range(k + 1, group):
                factor = columns[j][at : at + 1, :] * pivot
                columns[j] = jnp.where(sub1 == at, factor, columns[j] - columns[k] * factor)
    return block


def invert(ref, between=(), size=R, panel=32, group=16):
    hooks = dict(between)
    lane = lax.broadcasted_iota(jnp.int32, (size - panel, size), 1)

    def step(p, carry):
        block = sweep(ref[0:panel, :], group)
        rest = ref[panel:, :]
        update = jnp.dot(rest[:, 0:panel], block, preferred_element_type=F32, precision=HIGHEST)
        ref[0 : size - panel, :] = pltpu.roll(jnp.where(lane < panel, 0.0, rest) - update, size - panel, 1)
        ref[size - panel :, :] = pltpu.roll(block, size - panel, 1)
        return carry

    done = 0
    for p in sorted(set(hooks) | {size // panel - 1}):
        lax.fori_loop(done, p + 1, step, 0)
        done = p + 1
        if p in hooks:
            hooks[p]()


def eye(size=R):
    return (
        lax.broadcasted_iota(jnp.int32, (size, size), 0) == lax.broadcasted_iota(jnp.int32, (size, size), 1)
    ).astype(F32)


def gram(a, b):
    return lax.dot_general(a, b, (((0,), (0,)), ((), ())), preferred_element_type=F32)


def whole_kernel(
    owners, blocks, tile_contexts, count, item_ref, contexts, row_contexts, row_items, row_users, tile_users, values, profile, features,
    out, new,
    tab, fall, high, low, across_profile, part, sums,
    inv, passing, landed, outg, outf, pg, pf, cg, cf, sg, sf, xg, xf, tg, tf, zg, zf, yg, send_sem, recv_sem,
):
    z, x, c, y = position()
    yp, ym, y2 = neighbour(dy=1), neighbour(dy=-1), neighbour(dy=2)
    zp, zm, sib = neighbour(dz=1), neighbour(dz=-1), neighbour(dc=1)
    xs = [neighbour(dx=d) for d in range(1, NX)]
    zs = [neighbour(dz=d) for d in range(1, NZ)]
    other = lax.rem(c + 1, 2)
    barrier = greet([yp, ym, y2, sib, zp, zm] + xs)
    go = Sender(send_sem, recv_sem)
    later = {}
    tab[0:4] = item_ref[...]

    def own_part(i, carry):
        rows = pl.ds(pl.multiple_of(i * 256, 256), 256)
        product = jnp.dot(profile[rows, :], features[...], preferred_element_type=F32)
        part[0, rows, :] = product[:, :128]
        part[1, rows, :] = product[:, 128:]
        return carry

    lane128 = lax.broadcasted_iota(jnp.int32, (TR, CB), 1)
    lane16 = lax.broadcasted_iota(jnp.int32, (TR, IB), 1)
    sub16 = lax.broadcasted_iota(jnp.int32, (UB, TR), 0)

    def group_rows(g):
        return pl.ds(pl.multiple_of(g * GROUP, GROUP), GROUP)

    def tile_rows(at):
        return pl.ds(pl.multiple_of(at * TR, TR), TR)

    def context_rows(g, carry):
        key = jnp.transpose(row_contexts[group_rows(g), :])
        for t in range(GROUP):
            onehot = (jnp.broadcast_to(key[:, t : t + 1], (TR, CB)) == lane128).astype(F32).astype(BF16)
            at = g * GROUP + t
            block = contexts[tile_contexts[at]]
            high[tile_rows(at), :] = jnp.dot(onehot, block, preferred_element_type=F32).astype(BF16)
        return carry

    def turn(i, carry):
        rows = pl.ds(pl.multiple_of(i * 256, 256), 256)
        across_profile[:, rows] = jnp.transpose(profile[rows, :])
        return carry

    def idle(fn, first, last):
        lax.fori_loop(first, last, fn, 0)

    idle(own_part, 0, 8)
    idle(context_rows, 0, 1)
    barrier()

    def place(core, d, e, n=1):
        return tab.at[pl.ds(((core * NZ + d) * NX + e) * 4, 4 * n)]

    def up(s, e):
        return go(place(0, (-s) % 16, e), place(0, (-s - 1) % 16, e), zp)

    def down(s, e):
        return go(place(0, s, e), place(0, s + 1, e), zm)

    def share(d):
        return go(place(0, d, 0, 4), place(1, d, 0, 4), sib)

    own = place(0, 0, 0)
    arrivals = {3: go(own, place(0, 0, 3), xs[0]), 1: go(own, place(0, 0, 1), xs[2]), 2: go(own, place(0, 0, 2), xs[1])}
    ups, downs = {0: up(0, 0)}, {0: down(0, 0)}
    rows = pl.ds(pl.multiple_of(c * 256, 256), 256)
    feats = [
        go(features.at[rows], fall.at[pl.ds(512, 256)], yp),
        go(features.at[rows], fall.at[pl.ds(0, 256)], ym),
        go(features.at[rows], fall.at[pl.ds(256, 256)], y2),
    ]
    order = (0, 3, 1, 2)
    for e in order[1:]:
        arrivals[e].wait_recv()
        ups[e], downs[e] = up(0, e), down(0, e)
    shared = [share(0)]
    for s in range(8):
        if s < 7:
            idle(context_rows, s + 1, s + 2)
        idle(turn, s, s + 1)
        for e in order:
            if e in ups:
                ups.pop(e).wait_recv()
                if s < 6 or (s == 6 and e in (0, 3)):
                    ups[e] = up(s + 1, e)
            if e in downs:
                downs.pop(e).wait_recv()
                if s < 6 or (s == 6 and e in (1, 2)):
                    downs[e] = down(s + 1, e)
        shared.append(share(s + 1))
        if s < 7:
            shared.append(share(15 - s))
        if s == 5:
            for copy in feats:
                copy.wait_recv()
            shared.append(go(fall.at[pl.ds(0, 768)], fall.at[pl.ds(768, 768)], sib))
    for copy in shared:
        copy.wait_recv()

    def products(g, carry):
        key = jnp.transpose(row_items[group_rows(g), :])
        for t in range(GROUP):
            onehot = (jnp.broadcast_to(key[:, t : t + 1], (TR, IB)) == lane16).astype(F32).astype(BF16)
            at = g * GROUP + t
            block = tab[item_place(owners[at], blocks[at], z, x, c)]
            product = jnp.dot(onehot, block, preferred_element_type=F32) * high[tile_rows(at), :].astype(F32)
            top = product.astype(BF16)
            high[tile_rows(at), :] = top
            low[tile_rows(at), :] = (product - top.astype(F32)).astype(BF16)
        return carry

    lax.fori_loop(0, TILES // GROUP, products, 0)
    live = jnp.broadcast_to(count[...], (GROUP, TR))
    order16 = lax.broadcasted_iota(jnp.int32, (GROUP, TR), 0)
    to_block = (lax.broadcasted_iota(jnp.int32, (128, TILES), 0) == jnp.broadcast_to(tile_users[...], (128, TILES))).astype(F32)
    to_block = jnp.concatenate([to_block.astype(BF16)] * 3, axis=1)
    after, before, across = lax.rem(y + 1, NY), lax.rem(y + 3, NY), lax.rem(y + 2, NY)

    def top(q):
        return pl.ds(pl.multiple_of(q * 512, 512), 256)

    def bottom(q):
        return pl.ds(pl.multiple_of(q * 512 + 256, 256), 256)

    def add_tiles(h):
        columns = slice(h * 128, h * 128 + 128)

        def tile_sums(g, carry):
            user = row_users[group_rows(g), :]
            value = jnp.where(order16 + g * GROUP < live, values[group_rows(g), :].astype(F32), 0.0)
            for t in range(GROUP):
                at = g * GROUP + t
                weight = jnp.where(user[t : t + 1, :] == sub16, value[t : t + 1, :], 0.0).astype(BF16)
                sums[group_rows(at), :] = jnp.dot(
                    weight, high[tile_rows(at), columns], preferred_element_type=F32
                ) + jnp.dot(weight, low[tile_rows(at), columns], preferred_element_type=F32)
            return carry

        lax.fori_loop(0, TILES // GROUP, tile_sums, 0)
        for u in range(UB):
            rows = pl.ds(u, 128, stride=UB)
            value = sums[rows, :]
            first = value.astype(BF16)
            value = value - first.astype(F32)
            second = value.astype(BF16)
            third = (value - second.astype(F32)).astype(BF16)
            total = jnp.dot(to_block, jnp.concatenate([first, second, third], axis=0), preferred_element_type=F32)
            sums[rows, :] = total
        part[h] += sums[...]
        ap = go(part.at[h, top(across)], passing.at[h, 0], yp)
        am = go(part.at[h, bottom(across)], passing.at[h, 1], ym)
        bp = go(part.at[h, bottom(after)], landed.at[h, 0], yp)
        bm = go(part.at[h, top(before)], landed.at[h, 1], ym)

        def relay():
            ap.wait_recv()
            passing[h, 2] = passing[h, 0] + part[h, top(after), :]
            cp = go(passing.at[h, 2], landed.at[h, 2], yp)
            am.wait_recv()
            passing[h, 3] = passing[h, 1] + part[h, bottom(before), :]
            cm = go(passing.at[h, 3], landed.at[h, 3], ym)
            later[h] = (bm, cp, bp, cm)

        return relay

    relays = [add_tiles(0), add_tiles(1)]
    def item_gram(i, acc):
        rows = tab[pl.ds(pl.multiple_of(i * 64, 64), 64)].reshape(1024, R)
        return acc + gram(rows, rows)

    items = lax.fori_loop(0, 8, item_gram, jnp.zeros((R, R), F32))
    table = contexts[...].reshape(1024, R)
    relays[0]()
    normal = items * gram(table, table) + gram(features[...], features[...])
    inv[...] = normal + gram(fall[...], fall[...]) + RIDGE * eye()
    invert(inv, ((1, relays[1]),))

    def solve(rows, copies, one, two):
        total = jnp.zeros((256, R), F32)
        for h in range(2):
            for i in copies:
                later[h][i].wait_recv()
            right = part[h, rows, :] + landed[h, one] + landed[h, two]
            total = total + jnp.dot(
                right, inv[h * 128 : h * 128 + 128, :], preferred_element_type=F32, precision=HIGHEST
            )
        out[rows, :] = total.astype(BF16)

    solve(top(y), (0, 1), 1, 2)
    up0 = go(out.at[top(y)], out.at[top(y)], yp)
    um0 = go(out.at[top(y)], out.at[top(y)], ym)
    solve(bottom(y), (2, 3), 0, 3)
    um1 = go(out.at[bottom(y)], out.at[bottom(y)], ym)
    up1 = go(out.at[bottom(y)], out.at[bottom(y)], yp)

    def over_x(k, part, came, held, slots, rows):
        k.wait_recv()
        held[...] = (part[c] + came[...]).reshape(NX, rows, 128)
        return farthest_first(NX, lambda d: go(held.at[lax.rem(x + d, NX)], slots.at[d - 1], xs[d - 1]))

    def over_z(copies, held, slots, split, zslots, rows):
        total = held[x]
        for d, copy in enumerate(copies):
            copy.wait_recv()
            total = total + slots[d]
        for i in range(NZ):
            split[i] = total[i * rows : (i + 1) * rows, :]
        return farthest_first(NZ, lambda d: go(split.at[lax.rem(z + d, NZ)], zslots.at[d - 1], zs[d - 1]))

    def sum_z(copies, split, zslots):
        total = split[z]
        for d, copy in enumerate(copies):
            copy.wait_recv()
            total = total + zslots[d]
        return total

    def back_z(total, place):
        place[c, x, z] = total
        return farthest_first(NZ, lambda d: go(place.at[c, x, z], place.at[c, x, z], zs[d - 1]))

    def back_x(copies, place):
        for copy in copies:
            copy.wait_recv()
        return farthest_first(NX, lambda d: go(place.at[c, x], place.at[c, x], xs[d - 1]))

    def back_c(copies, place):
        for copy in copies:
            copy.wait_recv()
        return go(place.at[c], place.at[c], sib)

    mine = out[pl.ds(pl.multiple_of(y * 512, 512), 512), :]
    whole = gram(mine, mine)
    pg[0] = whole[:, :128]
    pg[1] = whole[:, 128:]
    kg = go(pg.at[other], cg, sib)
    ag = over_x(kg, pg, cg, sg, xg, 64)
    up0.wait_recv()
    vp = go(out.at[top(before)], out.at[top(before)], yp)
    bg = over_z(ag, sg, xg, tg, zg, 4)
    um0.wait_recv()
    um1.wait_recv()
    vm = go(out.at[bottom(after)], out.at[bottom(after)], ym)
    yg[0] = sum_z(bg, tg, zg)
    hy = [go(yg.at[0], yg.at[3], y2), go(yg.at[0], yg.at[1], yp), go(yg.at[0], yg.at[2], ym)]
    up1.wait_recv()
    vp.wait_recv()
    vm.wait_recv()
    whole = jnp.dot(across_profile[...], out[...], preferred_element_type=F32)
    pf[0] = whole[:, :128]
    pf[1] = whole[:, 128:]
    kf = go(pf.at[other], cf, sib)
    for copy in hy:
        copy.wait_recv()
    hg = back_z((yg[0] + yg[3]) + (yg[1] + yg[2]), outg)
    af = over_x(kf, pf, cf, sf, xf, 128)
    bf = over_z(af, sf, xf, tf, zf, 8)
    ig = back_x(hg, outg)
    back_c(ig, outg).wait_recv()
    for half in range(2):
        for i in range(NX):
            for j in range(NZ):
                at = i * 64 + j * 4
                inv[at : at + 4, half * 128 : (half + 1) * 128] = outg[half, i, j]
    inv[...] += RIDGE * eye()

    def third():
        later["z"] = back_z(sum_z(bf, tf, zf), outf)

    def fourth():
        later["x"] = back_x(later["z"], outf)

    def fifth():
        later["c"] = back_c(later["x"], outf)

    invert(inv, ((1, third), (4, fourth), (6, fifth)))
    later["c"].wait_recv()
    total = jnp.dot(outf[0].reshape(512, 128), inv[0:128, :], preferred_element_type=F32, precision=HIGHEST)
    total = total + jnp.dot(outf[1].reshape(512, 128), inv[128:, :], preferred_element_type=F32, precision=HIGHEST)
    new[...] = total.astype(BF16)
    go.finish()


def copy_kernel(uf, new, uf_out, new_out):
    uf_out[...] = uf[...]
    new_out[...] = new[...]


VM = pl.BlockSpec(memory_space=pltpu.VMEM)
SM = pl.BlockSpec(memory_space=pltpu.SMEM)


def remote_params(number):
    return pltpu.CompilerParams(collective_id=number, has_side_effects=True, vmem_limit_bytes=VMEM_LIMIT)


PLAIN = pltpu.CompilerParams(vmem_limit_bytes=VMEM_LIMIT)


def shape(dims, dtype):
    return jax.ShapeDtypeStruct(dims, dtype)


def sems(n):
    return [pltpu.SemaphoreType.DMA((n,)), pltpu.SemaphoreType.DMA((n,))]


def local(
    tile_users,
    tile_owners,
    tile_blocks,
    tile_contexts,
    row_users,
    row_items,
    row_contexts,
    tile_values,
    tile_count,
    item_factors,
    context_factors,
    profile,
    feature_factors,
):
    uf, new = tuple(
        pl.pallas_call(
            whole_kernel,
            out_shape=(shape((SLAB, R), BF16), shape((512, R), BF16)),
            in_specs=[SM] * 3 + [VM] * 10,
            out_specs=(VM, VM),
            scratch_shapes=[
                pltpu.VMEM((512, IB, R), BF16),
                pltpu.VMEM((1536, R), BF16),
                pltpu.VMEM((TILES * TR, R), BF16),
                pltpu.VMEM((TILES * TR, R), BF16),
                pltpu.VMEM((512, SLAB), BF16),
                pltpu.VMEM((2, SLAB, 128), F32),
                pltpu.VMEM((SLAB, 128), F32),
                pltpu.VMEM((R, R), F32),
                pltpu.VMEM((2, 4, 256, 128), F32),
                pltpu.VMEM((2, 4, 256, 128), F32),
                pltpu.VMEM((2, NX, NZ, 4, 128), F32),
                pltpu.VMEM((2, NX, NZ, 8, 128), F32),
                pltpu.VMEM((2, 256, 128), F32),
                pltpu.VMEM((2, 512, 128), F32),
                pltpu.VMEM((256, 128), F32),
                pltpu.VMEM((512, 128), F32),
                pltpu.VMEM((NX, 64, 128), F32),
                pltpu.VMEM((NX, 128, 128), F32),
                pltpu.VMEM((3, 64, 128), F32),
                pltpu.VMEM((3, 128, 128), F32),
                pltpu.VMEM((NZ, 4, 128), F32),
                pltpu.VMEM((NZ, 8, 128), F32),
                pltpu.VMEM((NZ - 1, 4, 128), F32),
                pltpu.VMEM((NZ - 1, 8, 128), F32),
                pltpu.VMEM((4, 4, 128), F32),
            ]
    + sems(200),
            compiler_params=remote_params(0),
            name="whole",
        )(
            tile_owners.reshape(TILES),
            tile_blocks.reshape(TILES),
            tile_contexts.reshape(TILES),
            tile_count,
            item_factors.reshape(4, IB, R),
            context_factors.reshape(8, CB, R),
            row_contexts.reshape(TILES, TR),
            row_items.reshape(TILES, TR),
            row_users.reshape(TILES, TR),
            tile_users.reshape(1, TILES),
            tile_values.reshape(TILES, TR),
            profile,
            feature_factors,
        )
    )
    return tuple(
        pl.pallas_call(
            copy_kernel,
            out_shape=(shape((SLAB, R), BF16), shape((512, R), BF16)),
            in_specs=[VM, VM],
            out_specs=(VM, VM),
            compiler_params=PLAIN,
            name="results",
        )(uf, new)
    )


def solution(mesh):
    in_specs = (
        P("users", "items", None),
        P("users", "items", None, None),
        P("users", "items", None),
        P("users", "items", None),
        P("users", "items", None, None),
        P("users", "items", None, None),
        P("users", "items", None, None),
        P("users", "items", None, None),
        P("users", "items"),
        P("users", None),
        P(),
        P("users", "items"),
        P("items", None),
    )
    out_specs = (P("users", None), P("items", None))
    return jax.shard_map(local, mesh=mesh, in_specs=in_specs, out_specs=out_specs, check_vma=False)
```
